128 devices in a mesh: row: 8 (over z, y_hi), col: 16 (over y_lo, x, core).
Axes of the slice: x: 4, y: 4 (y_hi: 2, y_lo: 2; y = y_hi * 2 + y_lo), z: 4, core: 2. Of those that a mesh axis runs over, the one named last changes fastest.
Arguments:
- object_amplitude: float32 [2048, 4096], P('row', 'col'), may hold values from 0.3 to 3
- object_phase: float32 [2048, 4096], P('row', 'col'), may hold values from -3.140625 to 3.140625
- probe: float32 [4, 2, 256, 256], replicated, may hold values from -6 to 6
- amplitudes: float32 [1024, 256, 256], P(('row', 'col')), may hold values from 0.5 to 3
- positions: int32 [1024, 2], P(('row', 'col')), may hold values from -64 to 64
Outputs:
- new_object: float32 [2, 2048, 4096], P(None, 'row', 'col')
- new_probe: float32 [4, 2, 256, 256], replicated
The draws below stay inside these ranges and needn't reach their ends.
Inputs may be any that keep to these rules, and one draw needn't show every extreme that they name: `positions`: row and column offsets of each frame's first pixel from the first pixel of its owner tile f // 8, tiles row-major; both ends of the range occur.
All inputs are finite; a program needn't handle non-finite values.
Results may differ from the reference program's by a relative error of at most 0.0014.
The reference program's roundings to bfloat16 on the way count: a program that leaves them out, or rounds other values in their place, can miss the bound.
Values sent between devices are 32-bit elements; how exact they have to be, the bound alone decides.
No kernel may reach another device: no remote copies, remote signals or barrier semaphores. Data moves between devices by JAX's collectives and lax.ppermute only.
A program may use at most 192 MiB of HBM per device.

```python
import math
import jax
import jax.numpy as jnp
from jax import lax

P_SIZE = 256
MODES = 4
TILE = 256
H = 64
FR_DEV = 8
FRAMES = 1024
NYO = 2048
NXO = 4096
N_ROW = 8
N_COL = 16


def place_ends(array, stream_key, low, top_value):
    longest = array.shape.index(max(array.shape))
    spots = []
    for shift in (0, 1):
        where = [jax.random.randint(jax.random.fold_in(stream_key, axis), (), 0, length) for axis, length in enumerate(array.shape)]
        where[longest] = (where[longest] + shift) % array.shape[longest]
        spots.append(tuple(where))
    return array.at[spots[0]].set(low).at[spots[1]].set(top_value)


def levels(stream_key, dims, shards, low, high):
    def one(axis_at, parts):
        steps = jax.random.uniform(jax.random.fold_in(jax.random.fold_in(stream_key, 6), axis_at), (parts,), jnp.float32, low / len(shards), high / len(shards))
        return jnp.repeat(jnp.exp(steps), dims[axis_at] // parts).reshape((-1,) + (1,) * (len(dims) - axis_at - 1))

    loudness = one(*shards[0])
    for cut in shards[1:]:
        loudness = loudness * one(*cut)
    return loudness


def centred(rng, dims, spread, reach, held_as=jnp.bfloat16):
    return jnp.clip(spread * jax.random.normal(rng, dims, jnp.float32), -reach, reach).astype(held_as)


def setup_inputs(seed: int = 0) -> dict:
    seeds = jax.random.split(jax.random.key(seed), 6)
    object_amplitude = jnp.clip(jnp.exp(math.log(3.0) - 2.3025851 * jax.random.uniform(seeds[0], (NYO, NXO), jnp.float32) ** levels(seeds[0], (NYO, NXO), ((0, 8), (1, 16)), -0.2, 0.2)), 0.3, 3.0)
    object_phase = jnp.clip(jax.random.uniform(seeds[1], (NYO, NXO), jnp.float32, -3.140625, 3.140625), -3.140625, 3.140625)
    probe = centred(seeds[2], (MODES, 2, P_SIZE, P_SIZE), 1.0, 6.0, jnp.float32)
    amplitudes = jnp.clip(0.5 + 2.5 * jax.random.uniform(seeds[3], (FRAMES, P_SIZE, P_SIZE), jnp.float32) ** levels(seeds[3], (FRAMES, P_SIZE, P_SIZE), ((0, 128),), -0.2, 0.2), 0.5, 3.0)
    positions = place_ends(jax.random.randint(seeds[4], (FRAMES, 2), 0 - H, TILE - P_SIZE + H + 1), jax.random.fold_in(seeds[4], 1), 0 - H, TILE - P_SIZE + H).astype(jnp.int32)
    return dict(object_amplitude=object_amplitude, object_phase=object_phase, probe=probe, amplitudes=amplitudes, positions=positions)


def fourier_table(frame_side, exponent_sign):
    counter = jnp.arange(frame_side, dtype=jnp.int32)
    product = counter[:, None] * counter[None, :] % frame_side
    phase_angle = product.astype(jnp.float32) * (2.0 * math.pi / frame_side)
    norming = 1.0 / math.sqrt(frame_side)
    real_part = jnp.cos(phase_angle) * norming
    imaginary = exponent_sign * jnp.sin(phase_angle) * norming
    upper_rows = jnp.stack([real_part, -imaginary], axis=1)
    lower_rows = jnp.stack([imaginary, real_part], axis=1)
    return jnp.stack([upper_rows, lower_rows], axis=0).astype(jnp.bfloat16)

def transform(matrix, values):
    wide = matrix.astype(jnp.float32)
    halfway = jnp.einsum('akcy,fmcyx->fmakx', wide, values.astype(jnp.float32), precision=lax.Precision.HIGHEST)
    halfway = lax.optimization_barrier(halfway.astype(jnp.bfloat16)).astype(jnp.float32)
    return jnp.einsum('fmakx,blax->fmbkl', halfway, wide, precision=lax.Precision.HIGHEST)

def frame_terms(patches, probe, measured, forward, inverse):
    object_real = patches[:, None, 0]
    object_imag = patches[:, None, 1]
    probe_real = probe[None, :, 0]
    probe_imag = probe[None, :, 1]
    exit_wave = jnp.stack([probe_real * object_real - probe_imag * object_imag, probe_real * object_imag + probe_imag * object_real], axis=2)
    spectrum = transform(forward, exit_wave.astype(jnp.bfloat16))
    intensity = lax.optimization_barrier(jnp.sum(spectrum * spectrum, axis=(1, 2)))
    factor = measured / jnp.maximum(jnp.sqrt(intensity), 1.0)
    corrected = (spectrum * factor[:, None, None]).astype(jnp.bfloat16)
    returned = transform(inverse, corrected)
    change = returned - exit_wave
    change_real = change[:, :, 0]
    change_imag = change[:, :, 1]
    object_gradient = jnp.stack([lax.optimization_barrier(jnp.sum(probe_real * change_real + probe_imag * change_imag, axis=1)), lax.optimization_barrier(jnp.sum(probe_real * change_imag - probe_imag * change_real, axis=1))], axis=1)
    probe_gradient = jnp.stack([lax.optimization_barrier(jnp.sum(object_real * change_real + object_imag * change_imag, axis=0)), lax.optimization_barrier(jnp.sum(object_real * change_imag - object_imag * change_real, axis=0))], axis=1)
    weight = lax.optimization_barrier(jnp.sum(patches * patches, axis=(0, 1)))
    return (object_gradient, probe_gradient, weight)

def reference(object_amplitude, object_phase, probe, amplitudes, positions):
    object_field = jnp.stack([object_amplitude * jnp.cos(object_phase), object_amplitude * jnp.sin(object_phase)])
    padded = jnp.pad(object_field, ((0, 0), (H, H), (H, H)))
    forward = fourier_table(P_SIZE, -1.0)
    inverse = fourier_table(P_SIZE, 1.0)
    blocks = N_ROW * N_COL
    measured_all = amplitudes.reshape(blocks, FR_DEV, P_SIZE, P_SIZE)
    offsets_all = positions.reshape(blocks, FR_DEV, 2)

    def one_block(running, inputs_here):
        gradient_sum, probe_total, weight_total = running
        block_index, measured, offsets = inputs_here
        tile_row = block_index // N_COL
        tile_col = block_index % N_COL
        anchor = jnp.stack([tile_row * TILE + H, tile_col * TILE + H]).astype(jnp.int32)
        starts = (offsets + anchor[None, :]).astype(jnp.int32)
        patches = jax.vmap(lambda start_pair: lax.dynamic_slice(padded, (jnp.int32(0), start_pair[0], start_pair[1]), (2, P_SIZE, P_SIZE)))(starts)
        object_gradient, probe_gradient, weight = frame_terms(patches, probe, measured, forward, inverse)

        def place_frame(counter, canvas):
            corner = starts[counter]
            current = lax.dynamic_slice(canvas, (jnp.int32(0), corner[0], corner[1]), (2, P_SIZE, P_SIZE))
            return lax.dynamic_update_slice(canvas, current + object_gradient[counter], (jnp.int32(0), corner[0], corner[1]))
        gradient_sum = lax.fori_loop(0, FR_DEV, place_frame, gradient_sum)
        return ((gradient_sum, probe_total + probe_gradient, weight_total + weight), None)
    initial = (jnp.zeros_like(padded), jnp.zeros((MODES, 2, P_SIZE, P_SIZE), jnp.float32), jnp.zeros((P_SIZE, P_SIZE), jnp.float32))
    (gradient_sum, probe_total, weight_total), unused = lax.scan(one_block, initial, (jnp.arange(blocks, dtype=jnp.int32), measured_all, offsets_all))
    new_probe = probe + probe_total / (weight_total + 1e-05)
    step_size = 1.0 / (jnp.max(lax.optimization_barrier(jnp.sum(probe * probe, axis=(0, 1)))) + 1e-06)
    new_object = object_field + gradient_sum[:, H:H + NYO, H:H + NXO] * step_size
    return (new_object, new_probe)
```

```python
import functools
import math

import jax
import jax.numpy as jnp
import numpy as np
from jax import lax
from jax.experimental import pallas as pl
from jax.experimental.pallas import tpu as pltpu
from jax.sharding import Mesh, PartitionSpec as P

H = 64
ROW = ("z", "yh")
COL = ("yl", "x", "c")
CHIPS = ("z", "yh", "yl", "x")
ALL = CHIPS + ("c",)
CHUNK = 16


def fourier_matrix(side):
    counter = np.arange(side, dtype=np.int64)
    angle = (counter[:, None] * counter[None, :] % side).astype(np.float64) * (2.0 * math.pi / side)
    norming = 1.0 / math.sqrt(side)
    real = np.cos(angle) * norming
    imag = -np.sin(angle) * norming
    whole = np.concatenate(
        [np.concatenate([real, -imag], axis=1), np.concatenate([imag, real], axis=1)], axis=0
    )
    return whole.astype(np.float32)


def placed(part, slide, shift, wide):
    rows, side = part.shape
    tall = jnp.concatenate([part, jnp.zeros((8, side), jnp.float32)], axis=0)
    tall = pltpu.roll(tall, slide, 0)
    tall = jnp.concatenate([tall, jnp.zeros((rows + 8, wide - side), jnp.float32)], axis=1)
    return pltpu.roll(tall, shift, 1)


def frames_kernel(
    starts_ref,
    step_ref,
    ext_ref,
    probe_ref,
    power_ref,
    amps_ref,
    fwd_ref,
    inv_ref,
    sums_ref,
    canvas_ref,
    field,
    patch,
    psib,
    half,
    spec,
    corr,
    canvas,
    total,
):
    f = pl.program_id(0)
    count = pl.num_programs(0)
    modes = probe_ref.shape[0] // 2
    side = probe_ref.shape[1]
    wide = ext_ref.shape[2]

    @pl.when(f == 0)
    def _():
        @pl.loop(0, wide // CHUNK)
        def _(i):
            rows = pl.ds(pl.multiple_of(i * CHUNK, CHUNK), CHUNK)
            amp = ext_ref[0, rows, :]
            phase = ext_ref[1, rows, :]
            field[0, rows, :] = amp * jnp.cos(phase)
            field[1, rows, :] = amp * jnp.sin(phase)
            canvas[0, rows, :] = jnp.zeros((CHUNK, wide), jnp.float32)
            canvas[1, rows, :] = jnp.zeros((CHUNK, wide), jnp.float32)

        for k in range(2):
            field[k, wide:, :] = jnp.zeros((8, wide), jnp.float32)
            canvas[k, wide:, :] = jnp.zeros((8, wide), jnp.float32)

        @pl.loop(0, side // CHUNK)
        def _(i):
            rows = pl.ds(pl.multiple_of(i * CHUNK, CHUNK), CHUNK)
            for p in range(2 * modes + 1):
                total[p, rows, :] = jnp.zeros((CHUNK, side), jnp.float32)

    r0 = starts_ref[2 * f] + H
    slide = lax.rem(r0, 8)
    base = pl.multiple_of(r0 - slide, 8)
    lift = lax.rem(CHUNK + 8 - slide, CHUNK + 8)
    c0 = starts_ref[2 * f + 1]
    back_shift = jnp.where(c0 > 0, wide - c0, -c0)
    fore_shift = jnp.where(c0 < 0, wide + c0, c0)

    for i in range(side // CHUNK):
        rows = slice(i * CHUNK, (i + 1) * CHUNK)
        o = [
            pltpu.roll(
                pltpu.roll(field[k, pl.ds(base + i * CHUNK, CHUNK + 8), :], back_shift, 1)[:, :side],
                lift,
                0,
            )[:CHUNK]
            for k in range(2)
        ]
        patch[0, rows, :] = o[0]
        patch[1, rows, :] = o[1]
        total[2 * modes, rows, :] += o[0] * o[0] + o[1] * o[1]
        for m in range(modes):
            pr = probe_ref[2 * m, rows, :]
            pi = probe_ref[2 * m + 1, rows, :]
            cols = slice(m * side, (m + 1) * side)
            psib[rows, cols] = (pr * o[0] - pi * o[1]).astype(jnp.bfloat16)
            psib[side + i * CHUNK : side + (i + 1) * CHUNK, cols] = (
                pr * o[1] + pi * o[0]
            ).astype(jnp.bfloat16)

    for m in range(modes):
        cols = slice(m * side, (m + 1) * side)
        h = jnp.dot(fwd_ref[...], psib[:, cols], preferred_element_type=jnp.float32)
        half[cols, :side] = h[:side].astype(jnp.bfloat16)
        half[cols, side:] = h[side:].astype(jnp.bfloat16)
    for m in range(modes):
        rows = slice(m * side, (m + 1) * side)
        spec[rows, :] = jnp.dot(half[rows, :], inv_ref[...], preferred_element_type=jnp.float32)
    for i in range(side // CHUNK):
        rows = slice(i * CHUNK, (i + 1) * CHUNK)
        parts = []
        energy = None
        for m in range(modes):
            row_m = slice(m * side + i * CHUNK, m * side + (i + 1) * CHUNK)
            a = spec[row_m, :side]
            b = spec[row_m, side:]
            e = a * a + b * b
            energy = e if energy is None else energy + e
            parts.append((a, b))
        fac = amps_ref[0, rows, :] * lax.rsqrt(jnp.maximum(energy, 1.0))
        for m in range(modes):
            cols = slice(m * side, (m + 1) * side)
            corr[rows, cols] = (parts[m][0] * fac).astype(jnp.bfloat16)
            corr[side + i * CHUNK : side + (i + 1) * CHUNK, cols] = (parts[m][1] * fac).astype(
                jnp.bfloat16
            )
    for m in range(modes):
        cols = slice(m * side, (m + 1) * side)
        h = jnp.dot(inv_ref[...], corr[:, cols], preferred_element_type=jnp.float32)
        half[cols, :side] = h[:side].astype(jnp.bfloat16)
        half[cols, side:] = h[side:].astype(jnp.bfloat16)
    for m in range(modes):
        rows = slice(m * side, (m + 1) * side)
        spec[rows, :] = jnp.dot(half[rows, :], fwd_ref[...], preferred_element_type=jnp.float32)
    for i in range(side // CHUNK):
        rows = slice(i * CHUNK, (i + 1) * CHUNK)
        o_r = patch[0, rows, :]
        o_i = patch[1, rows, :]
        power = power_ref[rows, :]
        g_r = -(o_r * power)
        g_i = -(o_i * power)
        for m in range(modes):
            row_m = slice(m * side + i * CHUNK, m * side + (i + 1) * CHUNK)
            a = spec[row_m, :side]
            b = spec[row_m, side:]
            pr = probe_ref[2 * m, rows, :]
            pi = probe_ref[2 * m + 1, rows, :]
            g_r += pr * a + pi * b
            g_i += pr * b - pi * a
            total[2 * m, rows, :] += o_r * a + o_i * b
            total[2 * m + 1, rows, :] += o_r * b - o_i * a
        here = pl.ds(base + i * CHUNK, CHUNK + 8)
        canvas[0, here, :] += placed(g_r, slide, fore_shift, wide)
        canvas[1, here, :] += placed(g_i, slide, fore_shift, wide)

    @pl.when(f == count - 1)
    def _():
        step = step_ref[0]

        @pl.loop(0, wide // CHUNK)
        def _(i):
            rows = pl.ds(pl.multiple_of(i * CHUNK, CHUNK), CHUNK)
            inside = jnp.logical_and(i * CHUNK >= H, i * CHUNK < H + side).astype(jnp.float32)
            for k in range(2):
                canvas_ref[k, rows, :side] = (
                    step * canvas[k, rows, :side] + inside * field[k, rows, :side]
                )
                canvas_ref[k, rows, side:] = step * canvas[k, rows, side:]

        planes = modes

        @pl.loop(0, side // 8)
        def _(i):
            rows = pl.ds(pl.multiple_of(i * 8, 8), 8)
            for j in range(side // 128):
                lanes = slice(j * 128, (j + 1) * 128)
                tile = i * (side // 128) + j
                for owner in range(2):
                    for p in range(planes):
                        sums_ref[owner, tile, p] = total[owner * planes + p, rows, lanes]
                    sums_ref[owner, tile, planes] = total[2 * modes, rows, lanes]


def frames(starts, step, ext, probe, power, amps, fwd, inv):
    count, side, _ = amps.shape
    planes = probe.shape[0]
    modes = planes // 2
    wide = ext.shape[2]
    tiles = (side // 8) * (side // 128)

    def whole(shape):
        return pl.BlockSpec(shape, lambda f, *_: (0,) * len(shape))

    return pl.pallas_call(
        frames_kernel,
        out_shape=(
            jax.ShapeDtypeStruct((2, tiles, planes // 2 + 1, 8, 128), jnp.float32),
            jax.ShapeDtypeStruct((2, wide, wide), jnp.float32),
        ),
        grid_spec=pltpu.PrefetchScalarGridSpec(
            num_scalar_prefetch=2,
            grid=(count,),
            in_specs=[
                whole((2, wide, wide)),
                whole((planes, side, side)),
                whole((side, side)),
                pl.BlockSpec((1, side, side), lambda f, *_: (f, 0, 0)),
                whole((2 * side, 2 * side)),
                whole((2 * side, 2 * side)),
            ],
            out_specs=(
                whole((2, tiles, planes // 2 + 1, 8, 128)),
                whole((2, wide, wide)),
            ),
            scratch_shapes=[
                pltpu.VMEM((2, wide + 8, wide), jnp.float32),
                pltpu.VMEM((2, side, side), jnp.float32),
                pltpu.VMEM((2 * side, modes * side), jnp.bfloat16),
                pltpu.VMEM((modes * side, 2 * side), jnp.bfloat16),
                pltpu.VMEM((modes * side, 2 * side), jnp.float32),
                pltpu.VMEM((2 * side, modes * side), jnp.bfloat16),
                pltpu.VMEM((2, wide + 8, wide), jnp.float32),
                pltpu.VMEM((planes + 1, side, side), jnp.float32),
            ],
        ),
        compiler_params=pltpu.CompilerParams(vmem_limit_bytes=48 * 1024 * 1024),
        cost_estimate=pl.CostEstimate(
            flops=count * modes * 4 * 8 * side**3, bytes_accessed=8 * 2**20, transcendentals=0
        ),
    )(starts, step, ext, probe, power, amps, fwd, inv)


def send(block, axes, shift):
    count = math.prod(lax.axis_size(a) for a in axes)
    return lax.ppermute(
        block, axes, [(i, i + shift) for i in range(count) if 0 <= i + shift < count]
    )


def shards(object_amplitude, object_phase, probe, amplitudes, positions):
    tile = object_amplitude.shape[0]
    side = probe.shape[2]
    own = jnp.stack([object_amplitude, object_phase])
    top = send(own[:, tile - H :], ROW, 1)
    bottom = send(own[:, :H], ROW, -1)
    tall = jnp.concatenate([top, own, bottom], axis=1)
    left = send(tall[:, :, tile - H :], COL, 1)
    right = send(tall[:, :, :H], COL, -1)
    ext = jnp.concatenate([tall, right, left], axis=2)

    power = jnp.sum(probe * probe, axis=(0, 1))
    step = 1.0 / (jnp.max(power) + 1e-06)
    table = fourier_matrix(side)
    planes = probe.reshape((-1, side, side))
    sums, canvas = frames(
        positions.reshape((-1,)),
        step.reshape((1,)),
        ext,
        planes,
        power,
        amplitudes,
        jnp.asarray(table, dtype=jnp.bfloat16),
        jnp.asarray(table.T, dtype=jnp.bfloat16),
    )

    core = lax.axis_index("c")
    mine = planes.shape[0] // 2
    other = lax.dynamic_index_in_dim(sums, 1 - core, 0, keepdims=False)
    kept = lax.dynamic_index_in_dim(sums, core, 0, keepdims=False)
    from_above = send(canvas[:, H + tile :, :], ROW, 1)
    from_below = send(canvas[:, :H, :], ROW, -1)
    both = kept + lax.ppermute(other, "c", [(0, 1), (1, 0)])
    spread = lax.all_to_all(both, CHIPS, 0, 0, tiled=True)
    summed = jnp.sum(spread, axis=0)
    chip = lax.axis_index(CHIPS)
    lanes = side // 128
    old = lax.dynamic_slice(
        planes, (core * mine, chip // lanes * 8, chip % lanes * 128), (mine, 8, 128)
    )
    weight = summed[mine]
    new = old + (summed[:mine] - old * weight) / (weight + 1e-05)
    centre = canvas[:, H : H + tile, :]
    centre = centre.at[:, :H].add(from_above)
    centre = centre.at[:, tile - H :].add(from_below)
    from_left = send(centre[:, :, tile : tile + H], COL, 1)
    from_right = send(centre[:, :, tile + H :], COL, -1)
    gathered = lax.all_to_all(
        jnp.broadcast_to(new[None], both.shape[:1] + new.shape), CHIPS, 0, 0, tiled=True
    )
    swapped = lax.ppermute(gathered, "c", [(0, 1), (1, 0)])
    first = jnp.where(core == 0, gathered, swapped)
    second = jnp.where(core == 0, swapped, gathered)
    pair = jnp.stack([first, second])
    pair = pair.reshape((2, side // 8, lanes, mine, 8, 128)).transpose((0, 3, 1, 4, 2, 5))
    new_probe = pair.reshape(probe.shape)
    inner = centre[:, :, :tile]
    inner = inner.at[:, :, :H].add(from_left)
    inner = inner.at[:, :, tile - H :].add(from_right)
    return (inner, new_probe)


def solution(mesh):
    fine = Mesh(mesh.devices.reshape((4, 2, 2, 4, 2)), ALL)
    in_specs = (
        P(ROW, COL),
        P(ROW, COL),
        P(),
        P(ALL, None, None),
        P(ALL, None),
    )
    out_specs = (P(None, ROW, COL), P())
    return jax.shard_map(shards, mesh=fine, in_specs=in_specs, out_specs=out_specs, check_vma=False)
```

```python
import functools
import math

import jax
import jax.numpy as jnp
import numpy as np
from jax import lax
from jax.experimental import pallas as pl
from jax.experimental.pallas import tpu as pltpu
from jax.sharding import Mesh, PartitionSpec as P

H = 64
ROW = ("z", "yh")
COL = ("yl", "x", "c")
CHIPS = ("z", "yh", "yl", "x")
ALL = CHIPS + ("c",)
CHUNK = 16
PATCH = 64


def real_form(table):
    return np.concatenate(
        [
            np.concatenate([table.real, -table.imag], axis=1),
            np.concatenate([table.imag, table.real], axis=1),
        ],
        axis=0,
    )


def fourier_tables(side):
    counter = np.arange(side, dtype=np.int64)
    angle = (counter[:, None] * counter[None, :] % side).astype(np.float64) * (2.0 * math.pi / side)
    table = (np.cos(angle) - 1j * np.sin(angle)) / math.sqrt(side)
    sorted_half = np.concatenate([counter[: side // 2 : 2], counter[1 : side // 2 : 2]])
    halves = table[sorted_half]
    row_fwd = np.stack([real_form(halves[:, p::2]) for p in range(2)])
    row_inv = np.stack([real_form(halves.conj()[:, p::2]) for p in range(2)])
    col_fwd = real_form(table).T
    col_inv = real_form(table.conj()).T
    return [jnp.asarray(t, dtype=jnp.bfloat16) for t in (row_fwd, col_fwd, row_inv, col_inv)]


def cosine_sine(angle):
    turns = jnp.floor(angle * (2.0 / math.pi) + 0.5)
    rest = ((angle - turns * 1.5703125) - turns * 4.837512969970703125e-4) - turns * 7.549789954e-8
    z = rest * rest
    s = ((-1.9515295891e-4 * z + 8.3321608736e-3) * z - 1.6666654611e-1) * z * rest + rest
    c = (
        ((2.443315711809948e-5 * z - 1.388731625493765e-3) * z + 4.166664568298827e-2) * z * z
        - 0.5 * z
        + 1.0
    )
    size = jnp.abs(turns)
    odd = size == 1.0
    sign = 1.0 - size
    return jnp.where(odd, -turns * s, sign * c), jnp.where(odd, turns * c, sign * s)


def frames_kernel(
    starts_ref,
    core_ref,
    step_ref,
    ext_ref,
    probe_ref,
    power_ref,
    amps_ref,
    row_fwd_ref,
    col_fwd_ref,
    row_inv_ref,
    col_inv_ref,
    kept_ref,
    other_ref,
    canvas_ref,
    field,
    patch,
    psib,
    half,
    spec,
    corr,
    canvas,
    total,
    lined,
    level,
):
    f = pl.program_id(0)
    count = pl.num_programs(0)
    modes = probe_ref.shape[0] // 2
    side = probe_ref.shape[1]
    wide = ext_ref.shape[2]
    hside = side // 2
    quarter = side // 4
    strips = wide // 128
    lines = wide // 2

    def strip_lanes(c):
        return slice(c * 128, (c + 1) * 128)

    @pl.when(f == 0)
    def _():
        zero = jnp.zeros((CHUNK, 128), jnp.float32)

        @pl.loop(0, wide // CHUNK)
        def _(i):
            rows = pl.ds(pl.multiple_of(i * CHUNK, CHUNK), CHUNK)
            for k in range(2):
                for c in range(strips):
                    lined[k, c, rows, :] = ext_ref[k, rows, strip_lanes(c)]

        @pl.loop(0, lines // CHUNK)
        def _(i):
            rows = pl.ds(pl.multiple_of(i * CHUNK, CHUNK), CHUNK)
            for p in range(2):
                source = pl.ds(2 * i * CHUNK + p, CHUNK, stride=2)
                for c in range(strips):
                    amp = lined[0, c, source, :]
                    cosine, sine = cosine_sine(lined[1, c, source, :])
                    for k, value in enumerate((amp * cosine, amp * sine)):
                        field[p, k, c + 1, rows, :] = value
                        if c == strips - 1:
                            field[p, k, 0, rows, :] = value
                for k in range(2):
                    for c in range(strips + 1):
                        canvas[p, k, c, rows, :] = zero

        for p in range(2):
            for k in range(2):
                for c in range(strips + 1):
                    field[p, k, c, lines:, :] = jnp.zeros((8, 128), jnp.float32)
                    canvas[p, k, c, lines:, :] = jnp.zeros((8, 128), jnp.float32)

        @pl.loop(0, side // CHUNK)
        def _(i):
            rows = pl.ds(pl.multiple_of(i * CHUNK, CHUNK), CHUNK)
            for p in range(2 * modes + 1):
                total[p, rows, :] = jnp.zeros((CHUNK, side), jnp.float32)

    r0 = starts_ref[2 * f] + H
    c0 = starts_ref[2 * f + 1]
    shift = jnp.where(c0 < 0, 128 + c0, c0)
    unshift = jnp.where(shift > 0, 128 - shift, 0)
    first = jnp.where(c0 < 0, 0, 1)
    lane_tall = lax.broadcasted_iota(jnp.int32, (PATCH + 8, 128), 1)

    for i in range(side // CHUNK):
        rows = slice(i * CHUNK, (i + 1) * CHUNK)
        for c in range(side // 128):
            level[c, rows, :] = amps_ref[0, rows, strip_lanes(c)]

    def cols(m):
        return slice(m * side, (m + 1) * side)

    def line_start(w):
        q = r0 + w
        index = q // 2
        slide = lax.rem(index, 8)
        return lax.rem(q, 2), pl.multiple_of(index - slide, 8), slide

    for w in range(2):
        p, base, slide = line_start(w)
        lift = lax.rem(PATCH + 8 - slide, PATCH + 8)
        for i in range(hside // PATCH):
            rows = slice(w * hside + i * PATCH, w * hside + (i + 1) * PATCH)
            o = []
            for k in range(2):
                turned = [
                    pltpu.roll(field[p, k, first + c, pl.ds(base + i * PATCH, PATCH + 8), :], unshift, 1)
                    for c in range(3)
                ]
                near = lane_tall < 128 - shift
                joined = [jnp.where(near, turned[c], turned[c + 1]) for c in range(2)]
                o.append(
                    jnp.concatenate([pltpu.roll(x, lift, 0)[:PATCH] for x in joined], axis=1)
                )
            patch[0, rows, :] = o[0]
            patch[1, rows, :] = o[1]
            total[2 * modes, rows, :] += o[0] * o[0] + o[1] * o[1]
            for m in range(modes):
                pr = probe_ref[2 * m, rows, :]
                pi = probe_ref[2 * m + 1, rows, :]
                psib[w, i * PATCH : (i + 1) * PATCH, cols(m)] = (pr * o[0] - pi * o[1]).astype(
                    jnp.bfloat16
                )
                psib[w, hside + i * PATCH : hside + (i + 1) * PATCH, cols(m)] = (
                    pr * o[1] + pi * o[0]
                ).astype(jnp.bfloat16)

    def butterfly(table, source, m):
        a = jnp.dot(table[0], source[0, :, cols(m)], preferred_element_type=jnp.float32)
        b = jnp.dot(table[1], source[1, :, cols(m)], preferred_element_type=jnp.float32)
        return (a + b).astype(jnp.bfloat16), (a - b).astype(jnp.bfloat16)

    for m in range(modes):
        for n, value in enumerate(butterfly(row_fwd_ref, psib, m)):
            rows = slice(m * side + n * hside, m * side + (n + 1) * hside)
            half[rows, :side] = value[:hside]
            half[rows, side:] = value[hside:]
    for m in range(modes):
        spec[cols(m), :] = jnp.dot(
            half[cols(m), :], col_fwd_ref[...], preferred_element_type=jnp.float32
        )
    for i in range(side // CHUNK):
        parts = []
        energy = None
        for m in range(modes):
            here = slice(m * side + i * CHUNK, m * side + (i + 1) * CHUNK)
            a = spec[here, :side]
            b = spec[here, side:]
            e = a * a + b * b
            energy = e if energy is None else energy + e
            parts.append((a, b))
        group, offset = divmod(i * CHUNK, quarter)
        parity = group % 2
        place = group // 2 * quarter + offset
        measured = jnp.concatenate(
            [level[c, pl.ds(parity + 2 * place, CHUNK, stride=2), :] for c in range(side // 128)],
            axis=1,
        )
        fac = measured * lax.rsqrt(jnp.maximum(energy, 1.0))
        for m in range(modes):
            corr[parity, place : place + CHUNK, cols(m)] = (parts[m][0] * fac).astype(jnp.bfloat16)
            corr[parity, hside + place : hside + place + CHUNK, cols(m)] = (
                parts[m][1] * fac
            ).astype(jnp.bfloat16)
    for m in range(modes):
        for n, value in enumerate(butterfly(row_inv_ref, corr, m)):
            for w in range(2):
                start = m * side + w * hside + n * quarter
                rows = slice(start, start + quarter)
                half[rows, :side] = value[w * quarter : (w + 1) * quarter]
                half[rows, side:] = value[hside + w * quarter : hside + (w + 1) * quarter]
    for m in range(modes):
        spec[cols(m), :] = jnp.dot(
            half[cols(m), :], col_inv_ref[...], preferred_element_type=jnp.float32
        )
    for w in range(2):
        p, base, slide = line_start(w)
        for i in range(hside // PATCH):
            rows = slice(w * hside + i * PATCH, w * hside + (i + 1) * PATCH)
            o_r = patch[0, rows, :]
            o_i = patch[1, rows, :]
            power = power_ref[rows, :]
            g_r = -(o_r * power)
            g_i = -(o_i * power)
            for m in range(modes):
                row_m = slice(
                    m * side + w * hside + i * PATCH, m * side + w * hside + (i + 1) * PATCH
                )
                a = spec[row_m, :side]
                b = spec[row_m, side:]
                pr = probe_ref[2 * m, rows, :]
                pi = probe_ref[2 * m + 1, rows, :]
                g_r += pr * a + pi * b
                g_i += pr * b - pi * a
                total[2 * m, rows, :] += o_r * a + o_i * b
                total[2 * m + 1, rows, :] += o_r * b - o_i * a
            here = pl.ds(base + i * PATCH, PATCH + 8)
            far = lane_tall >= shift
            none = jnp.zeros((8, 128), jnp.float32)
            for k, g in enumerate((g_r, g_i)):
                a, b = (
                    pltpu.roll(
                        pltpu.roll(jnp.concatenate([g[:, strip_lanes(c)], none], axis=0), slide, 0),
                        shift,
                        1,
                    )
                    for c in range(2)
                )
                canvas[p, k, first, here, :] += jnp.where(far, a, 0.0)
                canvas[p, k, first + 1, here, :] += jnp.where(far, b, a)
                canvas[p, k, first + 2, here, :] += jnp.where(far, 0.0, b)

    @pl.when(f == count - 1)
    def _():
        step = step_ref[0]

        @pl.loop(0, lines // CHUNK)
        def _(i):
            rows = pl.ds(pl.multiple_of(i * CHUNK, CHUNK), CHUNK)
            inside = jnp.logical_and(i * CHUNK >= H // 2, i * CHUNK < (H + side) // 2)
            inside = inside.astype(jnp.float32)
            for p in range(2):
                target = pl.ds(2 * i * CHUNK + p, CHUNK, stride=2)
                for k in range(2):
                    for c in range(strips):
                        value = canvas[p, k, c + 1, rows, :]
                        if c == strips - 1:
                            value = step * (value + canvas[p, k, 0, rows, :])
                        else:
                            value = step * value + inside * field[p, k, c + 1, rows, :]
                        lined[k, c, target, :] = value

        @pl.loop(0, wide // CHUNK)
        def _(i):
            rows = pl.ds(pl.multiple_of(i * CHUNK, CHUNK), CHUNK)
            for k in range(2):
                for c in range(strips):
                    canvas_ref[k, rows, strip_lanes(c)] = lined[k, c, rows, :]

        planes = modes
        mine = core_ref[0] * planes
        theirs = planes - mine

        @pl.loop(0, side // 8)
        def _(i):
            rows = pl.ds(pl.multiple_of(i * 8, 8), 8)
            for j in range(side // 128):
                lanes = slice(j * 128, (j + 1) * 128)
                tile = i * (side // 128) + j
                for p in range(planes):
                    kept_ref[tile, p] = total[mine + p, rows, lanes]
                    other_ref[tile, p] = total[theirs + p, rows, lanes]
                kept_ref[tile, planes] = total[2 * modes, rows, lanes]
                other_ref[tile, planes] = total[2 * modes, rows, lanes]


def assemble_kernel(core_ref, mine_ref, theirs_ref, out_ref, lined):
    p = pl.program_id(0)
    half = pl.num_programs(0) // 2
    side = out_ref.shape[1]
    lanes = side // 128
    plane = lax.rem(p, half)

    def place(source):
        for i in range(side // 8):
            parity, line = divmod(i * 8, side // 2)
            rows = pl.ds(2 * line + parity, 8, stride=2)
            for j in range(lanes):
                lined[j, rows, :] = source[i * lanes + j, plane]
        for i in range(side // 8):
            rows = slice(i * 8, (i + 1) * 8)
            for j in range(lanes):
                out_ref[0, rows, j * 128 : (j + 1) * 128] = lined[j, rows, :]

    is_mine = p // half == core_ref[0]

    @pl.when(is_mine)
    def _():
        place(mine_ref)

    @pl.when(jnp.logical_not(is_mine))
    def _():
        place(theirs_ref)


def assemble(core, mine, theirs, side):
    tiles, planes = mine.shape[:2]

    def whole(shape):
        return pl.BlockSpec(shape, lambda p, *_: (0,) * len(shape))

    return pl.pallas_call(
        assemble_kernel,
        out_shape=jax.ShapeDtypeStruct((2 * planes, side, side), jnp.float32),
        grid_spec=pltpu.PrefetchScalarGridSpec(
            num_scalar_prefetch=1,
            grid=(2 * planes,),
            in_specs=[whole(mine.shape), whole(theirs.shape)],
            out_specs=pl.BlockSpec((1, side, side), lambda p, *_: (p, 0, 0)),
            scratch_shapes=[pltpu.VMEM((side // 128, side, 128), jnp.float32)],
        ),
        compiler_params=pltpu.CompilerParams(vmem_limit_bytes=16 * 1024 * 1024),
        cost_estimate=pl.CostEstimate(flops=0, bytes_accessed=4 * 2**20, transcendentals=0),
    )(core, mine, theirs)


def frames(starts, core, step, ext, probe, power, amps, *tables):
    count, side, _ = amps.shape
    planes = probe.shape[0]
    modes = planes // 2
    wide = ext.shape[2]
    tiles = (side // 8) * (side // 128)

    def whole(shape):
        return pl.BlockSpec(shape, lambda f, *_: (0,) * len(shape))

    return pl.pallas_call(
        frames_kernel,
        out_shape=(
            jax.ShapeDtypeStruct((tiles, planes // 2 + 1, 8, 128), jnp.float32),
            jax.ShapeDtypeStruct((tiles, planes // 2 + 1, 8, 128), jnp.float32),
            jax.ShapeDtypeStruct((2, wide, wide), jnp.float32),
        ),
        grid_spec=pltpu.PrefetchScalarGridSpec(
            num_scalar_prefetch=3,
            grid=(count,),
            in_specs=[
                whole((2, wide, wide)),
                whole((planes, side, side)),
                whole((side, side)),
                pl.BlockSpec((1, side, side), lambda f, *_: (f, 0, 0)),
                *[whole(t.shape) for t in tables],
            ],
            out_specs=(
                whole((tiles, planes // 2 + 1, 8, 128)),
                whole((tiles, planes // 2 + 1, 8, 128)),
                whole((2, wide, wide)),
            ),
            scratch_shapes=[
                pltpu.VMEM((2, 2, wide // 128 + 1, wide // 2 + 8, 128), jnp.float32),
                pltpu.VMEM((2, side, side), jnp.float32),
                pltpu.VMEM((2, side, modes * side), jnp.bfloat16),
                pltpu.VMEM((modes * side, 2 * side), jnp.bfloat16),
                pltpu.VMEM((modes * side, 2 * side), jnp.float32),
                pltpu.VMEM((2, side, modes * side), jnp.bfloat16),
                pltpu.VMEM((2, 2, wide // 128 + 1, wide // 2 + 8, 128), jnp.float32),
                pltpu.VMEM((planes + 1, side, side), jnp.float32),
                pltpu.VMEM((2, wide // 128, wide, 128), jnp.float32),
                pltpu.VMEM((side // 128, side, 128), jnp.float32),
            ],
        ),
        compiler_params=pltpu.CompilerParams(vmem_limit_bytes=34 * 1024 * 1024),
        cost_estimate=pl.CostEstimate(
            flops=count * modes * 4 * 8 * side**3, bytes_accessed=8 * 2**20, transcendentals=0
        ),
    )(starts, core, step, ext, probe, power, amps, *tables)


def exchange(low, high, axes):
    count = math.prod(lax.axis_size(a) for a in axes)
    even = lax.axis_index(axes) % 2 == 0
    pairs = [(i, i + 1) for i in range(0, count - 1, 2)]
    gaps = [(i, i + 1) for i in range(1, count - 1, 2)]
    inner = lax.ppermute(
        jnp.where(even, high, low), axes, pairs + [(j, i) for i, j in pairs]
    )
    outer = lax.ppermute(jnp.where(even, low, high), axes, gaps + [(j, i) for i, j in gaps])
    return jnp.where(even, outer, inner), jnp.where(even, inner, outer)


def shards(object_amplitude, object_phase, probe, amplitudes, positions):
    tile = object_amplitude.shape[0]
    side = probe.shape[2]
    own = jnp.stack([object_amplitude, object_phase])
    top, bottom = exchange(own[:, :H], own[:, tile - H :], ROW)
    tall = jnp.concatenate([top, own, bottom], axis=1)
    left, right = exchange(tall[:, :, :H], tall[:, :, tile - H :], COL)
    ext = jnp.concatenate([tall, right, left], axis=2)

    planes = probe.reshape((-1, side // 2, 2, side)).swapaxes(1, 2).reshape((-1, side, side))
    power = jnp.sum(planes * planes, axis=0)
    step = 1.0 / (jnp.max(power) + 1e-06)
    core = lax.axis_index("c").astype(jnp.int32)
    kept, other, canvas = frames(
        positions.reshape((-1,)),
        core.reshape((1,)),
        step.reshape((1,)),
        ext,
        planes,
        power,
        amplitudes,
        *fourier_tables(side),
    )

    mine = planes.shape[0] // 2
    swap = [(0, 1), (1, 0)]
    both = kept + lax.ppermute(other, "c", swap)
    spread = lax.all_to_all(both, CHIPS, 0, 0, tiled=True)
    from_above, from_below = exchange(canvas[:, :H, :], canvas[:, H + tile :, :], ROW)
    spread, from_above, from_below = lax.optimization_barrier((spread, from_above, from_below))
    summed = jnp.sum(spread, axis=0)
    chip = lax.axis_index(CHIPS)
    lanes = side // 128
    old = lax.dynamic_slice(
        planes, (core * mine, chip // lanes * 8, chip % lanes * 128), (mine, 8, 128)
    )
    weight = summed[mine]
    new = old + (summed[:mine] - old * weight) / (weight + 1e-05)
    gathered = lax.all_to_all(
        jnp.broadcast_to(new[None], both.shape[:1] + new.shape), CHIPS, 0, 0, tiled=True
    )
    centre = canvas[:, H : H + tile, :]
    centre = centre.at[:, :H].add(from_above)
    centre = centre.at[:, tile - H :].add(from_below)
    from_left, from_right = exchange(centre[:, :, tile + H :], centre[:, :, tile : tile + H], COL)
    inner = centre[:, :, :tile]
    inner = inner.at[:, :, :H].add(from_left)
    inner = inner.at[:, :, tile - H :].add(from_right)
    gathered, inner = lax.optimization_barrier((gathered, inner))
    swapped = lax.ppermute(gathered, "c", swap)
    new_probe = assemble(core.reshape((1,)), gathered, swapped, side)
    return (inner, new_probe.reshape(probe.shape))


def solution(mesh):
    fine = Mesh(mesh.devices.reshape((4, 2, 2, 4, 2)), ALL)
    in_specs = (
        P(ROW, COL),
        P(ROW, COL),
        P(),
        P(ALL, None, None),
        P(ALL, None),
    )
    out_specs = (P(None, ROW, COL), P())
    return jax.shard_map(shards, mesh=fine, in_specs=in_specs, out_specs=out_specs, check_vma=False)
```

```python
import functools
import math

import jax
import jax.numpy as jnp
import numpy as np
from jax import lax
from jax.experimental import pallas as pl
from jax.experimental.pallas import tpu as pltpu
from jax.sharding import Mesh, PartitionSpec as P

H = 64
ROW = ("z", "yh")
COL = ("yl", "x", "c")
CHIPS = ("z", "yh", "yl", "x")
ALL = CHIPS + ("c",)
CHUNK = 16
PATCH = 64
GROUP = 64


def real_form(table):
    return np.concatenate(
        [
            np.concatenate([table.real, -table.imag], axis=1),
            np.concatenate([table.imag, table.real], axis=1),
        ],
        axis=0,
    )


def fourier_tables(side):
    counter = np.arange(side, dtype=np.int64)
    angle = (counter[:, None] * counter[None, :] % side).astype(np.float64) * (2.0 * math.pi / side)
    table = (np.cos(angle) - 1j * np.sin(angle)) / math.sqrt(side)
    sorted_half = np.concatenate([counter[: side // 2 : 2], counter[1 : side // 2 : 2]])
    halves = table[sorted_half]
    row_fwd = np.stack([real_form(halves[:, p::2]) for p in range(2)])
    row_inv = np.stack([real_form(halves.conj()[:, p::2]) for p in range(2)])
    col_fwd = real_form(table).T
    col_inv = real_form(table.conj()).T
    return [jnp.asarray(t, dtype=jnp.bfloat16) for t in (row_fwd, col_fwd, row_inv, col_inv)]


def cosine_sine(angle):
    turns = jnp.floor(angle * (2.0 / math.pi) + 0.5)
    rest = ((angle - turns * 1.5703125) - turns * 4.837512969970703125e-4) - turns * 7.549789954e-8
    z = rest * rest
    s = ((-1.9515295891e-4 * z + 8.3321608736e-3) * z - 1.6666654611e-1) * z * rest + rest
    c = (
        ((2.443315711809948e-5 * z - 1.388731625493765e-3) * z + 4.166664568298827e-2) * z * z
        - 0.5 * z
        + 1.0
    )
    size = jnp.abs(turns)
    odd = size == 1.0
    sign = 1.0 - size
    return jnp.where(odd, -turns * s, sign * c), jnp.where(odd, turns * c, sign * s)


def frames_kernel(
    starts_ref,
    core_ref,
    step_ref,
    ext_ref,
    probe_ref,
    power_ref,
    amps_ref,
    row_fwd_ref,
    col_fwd_ref,
    row_inv_ref,
    col_inv_ref,
    kept_ref,
    other_ref,
    canvas_ref,
    field,
    patch,
    psib,
    half,
    grad,
    corr,
    canvas,
    total,
    lined,
    level,
):
    f = pl.program_id(0)
    count = pl.num_programs(0)
    modes = probe_ref.shape[0] // 2
    side = probe_ref.shape[1]
    wide = ext_ref.shape[2]
    hside = side // 2
    quarter = side // 4
    strips = wide // 128
    lines = wide // 2

    def strip_lanes(c):
        return slice(c * 128, (c + 1) * 128)

    @pl.when(f == 0)
    def _():
        zero = jnp.zeros((CHUNK, 128), jnp.float32)

        @pl.loop(0, wide // CHUNK)
        def _(i):
            rows = pl.ds(pl.multiple_of(i * CHUNK, CHUNK), CHUNK)
            for k in range(2):
                for c in range(strips):
                    lined[k, c, rows, :] = ext_ref[k, rows, strip_lanes(c)]

        @pl.loop(0, lines // CHUNK)
        def _(i):
            rows = pl.ds(pl.multiple_of(i * CHUNK, CHUNK), CHUNK)
            for p in range(2):
                source = pl.ds(2 * i * CHUNK + p, CHUNK, stride=2)
                for c in range(strips):
                    amp = lined[0, c, source, :]
                    cosine, sine = cosine_sine(lined[1, c, source, :])
                    for k, value in enumerate((amp * cosine, amp * sine)):
                        field[p, k, c + 1, rows, :] = value
                        if c == strips - 1:
                            field[p, k, 0, rows, :] = value
                for k in range(2):
                    for c in range(strips + 1):
                        canvas[p, k, c, rows, :] = zero

        for p in range(2):
            for k in range(2):
                for c in range(strips + 1):
                    field[p, k, c, lines:, :] = jnp.zeros((8, 128), jnp.float32)
                    canvas[p, k, c, lines:, :] = jnp.zeros((8, 128), jnp.float32)

        @pl.loop(0, side // CHUNK)
        def _(i):
            rows = pl.ds(pl.multiple_of(i * CHUNK, CHUNK), CHUNK)
            for p in range(2 * modes + 1):
                total[p, rows, :] = jnp.zeros((CHUNK, side), jnp.float32)

    r0 = starts_ref[2 * f] + H
    c0 = starts_ref[2 * f + 1]
    shift = jnp.where(c0 < 0, 128 + c0, c0)
    unshift = jnp.where(shift > 0, 128 - shift, 0)
    first = jnp.where(c0 < 0, 0, 1)
    lane_tall = lax.broadcasted_iota(jnp.int32, (PATCH + 8, 128), 1)

    for i in range(side // CHUNK):
        rows = slice(i * CHUNK, (i + 1) * CHUNK)
        for c in range(side // 128):
            level[c, rows, :] = amps_ref[0, rows, strip_lanes(c)]

    def cols(m):
        return slice(m * side, (m + 1) * side)

    def line_start(w):
        q = r0 + w
        index = q // 2
        slide = lax.rem(index, 8)
        return lax.rem(q, 2), pl.multiple_of(index - slide, 8), slide

    for w in range(2):
        p, base, slide = line_start(w)
        lift = lax.rem(PATCH + 8 - slide, PATCH + 8)
        for i in range(hside // PATCH):
            rows = slice(w * hside + i * PATCH, w * hside + (i + 1) * PATCH)
            o = []
            for k in range(2):
                turned = [
                    pltpu.roll(field[p, k, first + c, pl.ds(base + i * PATCH, PATCH + 8), :], unshift, 1)
                    for c in range(3)
                ]
                near = lane_tall < 128 - shift
                joined = [jnp.where(near, turned[c], turned[c + 1]) for c in range(2)]
                o.append(
                    jnp.concatenate([pltpu.roll(x, lift, 0)[:PATCH] for x in joined], axis=1)
                )
            patch[0, rows, :] = o[0]
            patch[1, rows, :] = o[1]
            total[2 * modes, rows, :] += o[0] * o[0] + o[1] * o[1]
            for m in range(modes):
                pr = probe_ref[2 * m, rows, :]
                pi = probe_ref[2 * m + 1, rows, :]
                psib[w, i * PATCH : (i + 1) * PATCH, cols(m)] = (pr * o[0] - pi * o[1]).astype(
                    jnp.bfloat16
                )
                psib[w, hside + i * PATCH : hside + (i + 1) * PATCH, cols(m)] = (
                    pr * o[1] + pi * o[0]
                ).astype(jnp.bfloat16)

    def butterfly(table, source, m):
        a = jnp.dot(table[0], source[0, :, cols(m)], preferred_element_type=jnp.float32)
        b = jnp.dot(table[1], source[1, :, cols(m)], preferred_element_type=jnp.float32)
        return (a + b).astype(jnp.bfloat16), (a - b).astype(jnp.bfloat16)

    def spread_rows(m, row, lanes, value):
        size = min(GROUP, value.shape[0])
        for t in range(value.shape[0] // size):
            group, offset = divmod(row + t * size, GROUP)
            start = (group * modes + m) * GROUP + offset
            half[start : start + size, lanes] = value[t * size : (t + 1) * size]

    def columns(t, table):
        rows = slice(t * modes * GROUP, (t + 1) * modes * GROUP)
        return jnp.dot(half[rows, :], table[...], preferred_element_type=jnp.float32)

    first_lanes, last_lanes = slice(0, side), slice(side, 2 * side)
    for m in range(modes):
        for n, value in enumerate(butterfly(row_fwd_ref, psib, m)):
            spread_rows(m, n * hside, first_lanes, value[:hside])
            spread_rows(m, n * hside, last_lanes, value[hside:])
    for t in range(side // GROUP):
        product = columns(t, col_fwd_ref)
        for u in range(GROUP // CHUNK):
            i = t * (GROUP // CHUNK) + u
            parts = []
            energy = None
            for m in range(modes):
                here = slice(m * GROUP + u * CHUNK, m * GROUP + (u + 1) * CHUNK)
                a = product[here, :side]
                b = product[here, side:]
                e = a * a + b * b
                energy = e if energy is None else energy + e
                parts.append((a, b))
            group, offset = divmod(i * CHUNK, quarter)
            parity = group % 2
            place = group // 2 * quarter + offset
            measured = jnp.concatenate(
                [level[c, pl.ds(parity + 2 * place, CHUNK, stride=2), :] for c in range(side // 128)],
                axis=1,
            )
            fac = measured * lax.rsqrt(jnp.maximum(energy, 1.0))
            for m in range(modes):
                corr[parity, place : place + CHUNK, cols(m)] = (parts[m][0] * fac).astype(
                    jnp.bfloat16
                )
                corr[parity, hside + place : hside + place + CHUNK, cols(m)] = (
                    parts[m][1] * fac
                ).astype(jnp.bfloat16)
    for m in range(modes):
        for n, value in enumerate(butterfly(row_inv_ref, corr, m)):
            for w in range(2):
                row = w * hside + n * quarter
                spread_rows(m, row, first_lanes, value[w * quarter : (w + 1) * quarter])
                spread_rows(
                    m, row, last_lanes, value[hside + w * quarter : hside + (w + 1) * quarter]
                )
    for t in range(side // GROUP):
        product = columns(t, col_inv_ref)
        for u in range(GROUP // CHUNK):
            rows = slice(t * GROUP + u * CHUNK, t * GROUP + (u + 1) * CHUNK)
            o_r = patch[0, rows, :]
            o_i = patch[1, rows, :]
            power = power_ref[rows, :]
            g_r = -(o_r * power)
            g_i = -(o_i * power)
            for m in range(modes):
                here = slice(m * GROUP + u * CHUNK, m * GROUP + (u + 1) * CHUNK)
                a = product[here, :side]
                b = product[here, side:]
                pr = probe_ref[2 * m, rows, :]
                pi = probe_ref[2 * m + 1, rows, :]
                g_r += pr * a + pi * b
                g_i += pr * b - pi * a
                total[2 * m, rows, :] += o_r * a + o_i * b
                total[2 * m + 1, rows, :] += o_r * b - o_i * a
            grad[0, rows, :] = g_r
            grad[1, rows, :] = g_i
    for w in range(2):
        p, base, slide = line_start(w)
        for i in range(hside // PATCH):
            rows = slice(w * hside + i * PATCH, w * hside + (i + 1) * PATCH)
            here = pl.ds(base + i * PATCH, PATCH + 8)
            far = lane_tall >= shift
            none = jnp.zeros((8, 128), jnp.float32)
            for k in range(2):
                a, b = (
                    pltpu.roll(
                        pltpu.roll(
                            jnp.concatenate([grad[k, rows, strip_lanes(c)], none], axis=0), slide, 0
                        ),
                        shift,
                        1,
                    )
                    for c in range(2)
                )
                canvas[p, k, first, here, :] += jnp.where(far, a, 0.0)
                canvas[p, k, first + 1, here, :] += jnp.where(far, b, a)
                canvas[p, k, first + 2, here, :] += jnp.where(far, 0.0, b)

    @pl.when(f == count - 1)
    def _():
        step = step_ref[0]

        @pl.loop(0, lines // CHUNK)
        def _(i):
            rows = pl.ds(pl.multiple_of(i * CHUNK, CHUNK), CHUNK)
            inside = jnp.logical_and(i * CHUNK >= H // 2, i * CHUNK < (H + side) // 2)
            inside = inside.astype(jnp.float32)
            for p in range(2):
                target = pl.ds(2 * i * CHUNK + p, CHUNK, stride=2)
                for k in range(2):
                    for c in range(strips):
                        value = canvas[p, k, c + 1, rows, :]
                        if c == strips - 1:
                            value = step * (value + canvas[p, k, 0, rows, :])
                        else:
                            value = step * value + inside * field[p, k, c + 1, rows, :]
                        lined[k, c, target, :] = value

        @pl.loop(0, wide // CHUNK)
        def _(i):
            rows = pl.ds(pl.multiple_of(i * CHUNK, CHUNK), CHUNK)
            for k in range(2):
                for c in range(strips):
                    canvas_ref[k, rows, strip_lanes(c)] = lined[k, c, rows, :]

        planes = modes
        mine = core_ref[0] * planes
        theirs = planes - mine

        @pl.loop(0, side // 8)
        def _(i):
            rows = pl.ds(pl.multiple_of(i * 8, 8), 8)
            for j in range(side // 128):
                lanes = slice(j * 128, (j + 1) * 128)
                tile = i * (side // 128) + j
                for p in range(planes):
                    kept_ref[tile, p] = total[mine + p, rows, lanes]
                    other_ref[tile, p] = total[theirs + p, rows, lanes]
                kept_ref[tile, planes] = total[2 * modes, rows, lanes]
                other_ref[tile, planes] = total[2 * modes, rows, lanes]


def renew_kernel(spread_ref, old_ref, out_ref):
    modes = old_ref.shape[0]
    sums = [jnp.zeros((8, 128), jnp.float32) for _ in range(modes + 1)]
    for i in range(spread_ref.shape[0]):
        for p in range(modes + 1):
            sums[p] += spread_ref[i, p]
    weight = sums[modes]
    for p in range(modes):
        old = old_ref[p]
        new = old + (sums[p] - old * weight) / (weight + 1e-05)
        for i in range(out_ref.shape[0]):
            out_ref[i, p] = new


def renew(spread, old):
    return pl.pallas_call(
        renew_kernel,
        out_shape=jax.ShapeDtypeStruct(spread.shape[:1] + old.shape, jnp.float32),
        in_specs=[pl.BlockSpec(memory_space=pltpu.VMEM)] * 2,
        out_specs=pl.BlockSpec(memory_space=pltpu.VMEM),
        compiler_params=pltpu.CompilerParams(vmem_limit_bytes=8 * 1024 * 1024),
        cost_estimate=pl.CostEstimate(flops=0, bytes_accessed=2 * 2**20, transcendentals=0),
    )(spread, old)


def assemble_kernel(first_ref, source_ref, *refs):
    out_ref, lined = refs[-2:]
    plane = pl.program_id(0)
    side = out_ref.shape[1]
    lanes = side // 128
    for i in range(side // 8):
        parity, line = divmod(i * 8, side // 2)
        rows = pl.ds(2 * line + parity, 8, stride=2)
        for j in range(lanes):
            lined[j, rows, :] = source_ref[i * lanes + j, plane]
    for i in range(side // 8):
        rows = slice(i * 8, (i + 1) * 8)
        for j in range(lanes):
            out_ref[0, rows, j * 128 : (j + 1) * 128] = lined[j, rows, :]


def assemble(first, source, side, started=None):
    planes = source.shape[1]
    more = () if started is None else (started,)
    return pl.pallas_call(
        assemble_kernel,
        out_shape=jax.ShapeDtypeStruct((2 * planes, side, side), jnp.float32),
        grid_spec=pltpu.PrefetchScalarGridSpec(
            num_scalar_prefetch=1,
            grid=(planes,),
            in_specs=[
                pl.BlockSpec(source.shape, lambda p, *_: (0,) * source.ndim),
                *[pl.BlockSpec(memory_space=pl.ANY) for _ in more],
            ],
            out_specs=pl.BlockSpec(
                (1, side, side), lambda p, first_ref: (first_ref[0] + p, 0, 0)
            ),
            scratch_shapes=[pltpu.VMEM((side // 128, side, 128), jnp.float32)],
        ),
        input_output_aliases={2: 0} if more else {},
        compiler_params=pltpu.CompilerParams(vmem_limit_bytes=16 * 1024 * 1024),
        cost_estimate=pl.CostEstimate(flops=0, bytes_accessed=2 * 2**20, transcendentals=0),
    )(first, source, *more)


def frames(starts, core, step, ext, probe, power, amps, *tables):
    count, side, _ = amps.shape
    planes = probe.shape[0]
    modes = planes // 2
    wide = ext.shape[2]
    tiles = (side // 8) * (side // 128)

    def whole(shape):
        return pl.BlockSpec(shape, lambda f, *_: (0,) * len(shape))

    return pl.pallas_call(
        frames_kernel,
        out_shape=(
            jax.ShapeDtypeStruct((tiles, planes // 2 + 1, 8, 128), jnp.float32),
            jax.ShapeDtypeStruct((tiles, planes // 2 + 1, 8, 128), jnp.float32),
            jax.ShapeDtypeStruct((2, wide, wide), jnp.float32),
        ),
        grid_spec=pltpu.PrefetchScalarGridSpec(
            num_scalar_prefetch=3,
            grid=(count,),
            in_specs=[
                whole((2, wide, wide)),
                whole((planes, side, side)),
                whole((side, side)),
                pl.BlockSpec((1, side, side), lambda f, *_: (f, 0, 0)),
                *[whole(t.shape) for t in tables],
            ],
            out_specs=(
                whole((tiles, planes // 2 + 1, 8, 128)),
                whole((tiles, planes // 2 + 1, 8, 128)),
                whole((2, wide, wide)),
            ),
            scratch_shapes=[
                pltpu.VMEM((2, 2, wide // 128 + 1, wide // 2 + 8, 128), jnp.float32),
                pltpu.VMEM((2, side, side), jnp.float32),
                pltpu.VMEM((2, side, modes * side), jnp.bfloat16),
                pltpu.VMEM((modes * side, 2 * side), jnp.bfloat16),
                pltpu.VMEM((2, side, side), jnp.float32),
                pltpu.VMEM((2, side, modes * side), jnp.bfloat16),
                pltpu.VMEM((2, 2, wide // 128 + 1, wide // 2 + 8, 128), jnp.float32),
                pltpu.VMEM((planes + 1, side, side), jnp.float32),
                pltpu.VMEM((2, wide // 128, wide, 128), jnp.float32),
                pltpu.VMEM((side // 128, side, 128), jnp.float32),
            ],
        ),
        compiler_params=pltpu.CompilerParams(vmem_limit_bytes=34 * 1024 * 1024),
        cost_estimate=pl.CostEstimate(
            flops=count * modes * 4 * 8 * side**3, bytes_accessed=8 * 2**20, transcendentals=0
        ),
    )(starts, core, step, ext, probe, power, amps, *tables)


def exchange(low, high, axes):
    count = math.prod(lax.axis_size(a) for a in axes)
    even = lax.axis_index(axes) % 2 == 0
    pairs = [(i, i + 1) for i in range(0, count - 1, 2)]
    gaps = [(i, i + 1) for i in range(1, count - 1, 2)]
    inner = lax.ppermute(
        jnp.where(even, high, low), axes, pairs + [(j, i) for i, j in pairs]
    )
    outer = lax.ppermute(jnp.where(even, low, high), axes, gaps + [(j, i) for i, j in gaps])
    return jnp.where(even, outer, inner), jnp.where(even, inner, outer)


def shards(object_amplitude, object_phase, probe, amplitudes, positions):
    tile = object_amplitude.shape[0]
    side = probe.shape[2]
    own = jnp.stack([object_amplitude, object_phase])
    top, bottom = exchange(own[:, :H], own[:, tile - H :], ROW)
    tall = jnp.concatenate([top, own, bottom], axis=1)
    left, right = exchange(tall[:, :, :H], tall[:, :, tile - H :], COL)
    ext = jnp.concatenate([tall, right, left], axis=2)

    planes = probe.reshape((-1, side // 2, 2, side)).swapaxes(1, 2).reshape((-1, side, side))
    power = jnp.sum(planes * planes, axis=0)
    step = 1.0 / (jnp.max(power) + 1e-06)
    core = lax.axis_index("c").astype(jnp.int32)
    kept, other, canvas = frames(
        positions.reshape((-1,)),
        core.reshape((1,)),
        step.reshape((1,)),
        ext,
        planes,
        power,
        amplitudes,
        *fourier_tables(side),
    )

    mine = planes.shape[0] // 2
    swap = [(0, 1), (1, 0)]
    both = kept + lax.ppermute(other, "c", swap)
    from_above, from_below = exchange(canvas[:, :H, :], canvas[:, H + tile :, :], ROW)
    both, from_above, from_below = lax.optimization_barrier((both, from_above, from_below))
    spread = lax.all_to_all(both, CHIPS, 0, 0, tiled=True)
    chip = lax.axis_index(CHIPS)
    lanes = side // 128
    old = lax.dynamic_slice(
        planes, (core * mine, chip // lanes * 8, chip % lanes * 128), (mine, 8, 128)
    )
    gathered = lax.all_to_all(renew(spread, old), CHIPS, 0, 0, tiled=True)
    centre = canvas[:, H : H + tile, :]
    centre = centre.at[:, :H].add(from_above)
    centre = centre.at[:, tile - H :].add(from_below)
    from_left, from_right = exchange(centre[:, :, tile + H :], centre[:, :, tile : tile + H], COL)
    inner = centre[:, :, :tile]
    inner = inner.at[:, :, :H].add(from_left)
    inner = inner.at[:, :, tile - H :].add(from_right)
    gathered, inner = lax.optimization_barrier((gathered, inner))
    swapped = lax.ppermute(gathered, "c", swap)
    first = (core * mine).reshape((1,))
    new_probe = assemble(first, gathered, side)
    new_probe = assemble(mine - first, swapped, side, new_probe)
    return (inner, new_probe.reshape(probe.shape))


def solution(mesh):
    fine = Mesh(mesh.devices.reshape((4, 2, 2, 4, 2)), ALL)
    in_specs = (
        P(ROW, COL),
        P(ROW, COL),
        P(),
        P(ALL, None, None),
        P(ALL, None),
    )
    out_specs = (P(None, ROW, COL), P())
    return jax.shard_map(shards, mesh=fine, in_specs=in_specs, out_specs=out_specs, check_vma=False)
```

```python
import functools
import math

import jax
import jax.numpy as jnp
import numpy as np
from jax import lax
from jax.experimental import pallas as pl
from jax.experimental.pallas import tpu as pltpu
from jax.sharding import Mesh, PartitionSpec as P

H = 64
ROW = ("z", "yh")
COL = ("yl", "x", "c")
CHIPS = ("z", "yh", "yl", "x")
ALL = CHIPS + ("c",)
CHUNK = 16
PATCH = 64
GROUP = 64


def real_form(table):
    return np.concatenate(
        [
            np.concatenate([table.real, -table.imag], axis=1),
            np.concatenate([table.imag, table.real], axis=1),
        ],
        axis=0,
    )


def fourier_tables(side):
    counter = np.arange(side, dtype=np.int64)
    angle = (counter[:, None] * counter[None, :] % side).astype(np.float64) * (2.0 * math.pi / side)
    table = (np.cos(angle) - 1j * np.sin(angle)) / math.sqrt(side)
    sorted_half = np.concatenate([counter[: side // 2 : 2], counter[1 : side // 2 : 2]])
    halves = table[sorted_half]
    row_fwd = np.stack([real_form(halves[:, p::2]) for p in range(2)])
    row_inv = np.stack([real_form(halves.conj()[:, p::2]) for p in range(2)])
    col_fwd = real_form(table).T
    col_inv = real_form(table.conj()).T
    return [jnp.asarray(t, dtype=jnp.bfloat16) for t in (row_fwd, col_fwd, row_inv, col_inv)]


def cosine_sine(angle):
    turns = jnp.floor(angle * (2.0 / math.pi) + 0.5)
    rest = ((angle - turns * 1.5703125) - turns * 4.837512969970703125e-4) - turns * 7.549789954e-8
    z = rest * rest
    s = ((-1.9515295891e-4 * z + 8.3321608736e-3) * z - 1.6666654611e-1) * z * rest + rest
    c = (
        ((2.443315711809948e-5 * z - 1.388731625493765e-3) * z + 4.166664568298827e-2) * z * z
        - 0.5 * z
        + 1.0
    )
    size = jnp.abs(turns)
    odd = size == 1.0
    sign = 1.0 - size
    return jnp.where(odd, -turns * s, sign * c), jnp.where(odd, turns * c, sign * s)


def frames_kernel(
    starts_ref,
    core_ref,
    step_ref,
    ext_ref,
    probe_ref,
    power_ref,
    amps_ref,
    row_fwd_ref,
    col_fwd_ref,
    row_inv_ref,
    col_inv_ref,
    kept_ref,
    other_ref,
    canvas_ref,
    field,
    patch,
    psib,
    half,
    grad,
    corr,
    canvas,
    total,
    lined,
    level,
):
    f = pl.program_id(0)
    count = pl.num_programs(0)
    modes = probe_ref.shape[0] // 2
    side = probe_ref.shape[1]
    wide = ext_ref.shape[2]
    hside = side // 2
    quarter = side // 4
    strips = wide // 128
    lines = wide // 2

    def strip_lanes(c):
        return slice(c * 128, (c + 1) * 128)

    @pl.when(f == 0)
    def _():
        zero = jnp.zeros((CHUNK, 128), jnp.float32)

        @pl.loop(0, wide // CHUNK)
        def _(i):
            rows = pl.ds(pl.multiple_of(i * CHUNK, CHUNK), CHUNK)
            for k in range(2):
                for c in range(strips):
                    lined[k, c, rows, :] = ext_ref[k, rows, strip_lanes(c)]

        @pl.loop(0, lines // CHUNK)
        def _(i):
            rows = pl.ds(pl.multiple_of(i * CHUNK, CHUNK), CHUNK)
            for p in range(2):
                source = pl.ds(2 * i * CHUNK + p, CHUNK, stride=2)
                for c in range(strips):
                    amp = lined[0, c, source, :]
                    cosine, sine = cosine_sine(lined[1, c, source, :])
                    for k, value in enumerate((amp * cosine, amp * sine)):
                        field[p, k, c + 1, rows, :] = value
                        if c == strips - 1:
                            field[p, k, 0, rows, :] = value
                for k in range(2):
                    for c in range(strips + 1):
                        canvas[p, k, c, rows, :] = zero

        for p in range(2):
            for k in range(2):
                for c in range(strips + 1):
                    field[p, k, c, lines:, :] = jnp.zeros((8, 128), jnp.float32)
                    canvas[p, k, c, lines:, :] = jnp.zeros((8, 128), jnp.float32)

        @pl.loop(0, side // CHUNK)
        def _(i):
            rows = pl.ds(pl.multiple_of(i * CHUNK, CHUNK), CHUNK)
            for p in range(2 * modes + 1):
                total[p, rows, :] = jnp.zeros((CHUNK, side), jnp.float32)

    r0 = starts_ref[2 * f] + H
    c0 = starts_ref[2 * f + 1]
    shift = jnp.where(c0 < 0, 128 + c0, c0)
    unshift = jnp.where(shift > 0, 128 - shift, 0)
    first = jnp.where(c0 < 0, 0, 1)
    lane_tall = lax.broadcasted_iota(jnp.int32, (PATCH + 8, 128), 1)

    for i in range(side // CHUNK):
        rows = slice(i * CHUNK, (i + 1) * CHUNK)
        for c in range(side // 128):
            level[c, rows, :] = amps_ref[0, rows, strip_lanes(c)]

    def cols(m):
        return slice(m * side, (m + 1) * side)

    def line_start(w):
        q = r0 + w
        index = q // 2
        slide = lax.rem(index, 8)
        return lax.rem(q, 2), pl.multiple_of(index - slide, 8), slide

    for w in range(2):
        p, base, slide = line_start(w)
        lift = lax.rem(PATCH + 8 - slide, PATCH + 8)
        for i in range(hside // PATCH):
            rows = slice(w * hside + i * PATCH, w * hside + (i + 1) * PATCH)
            o = []
            for k in range(2):
                turned = [
                    pltpu.roll(field[p, k, first + c, pl.ds(base + i * PATCH, PATCH + 8), :], unshift, 1)
                    for c in range(3)
                ]
                near = lane_tall < 128 - shift
                joined = [jnp.where(near, turned[c], turned[c + 1]) for c in range(2)]
                o.append(
                    jnp.concatenate([pltpu.roll(x, lift, 0)[:PATCH] for x in joined], axis=1)
                )
            patch[0, rows, :] = o[0]
            patch[1, rows, :] = o[1]
            total[2 * modes, rows, :] += o[0] * o[0] + o[1] * o[1]
            for m in range(modes):
                pr = probe_ref[2 * m, rows, :]
                pi = probe_ref[2 * m + 1, rows, :]
                psib[w, i * PATCH : (i + 1) * PATCH, cols(m)] = (pr * o[0] - pi * o[1]).astype(
                    jnp.bfloat16
                )
                psib[w, hside + i * PATCH : hside + (i + 1) * PATCH, cols(m)] = (
                    pr * o[1] + pi * o[0]
                ).astype(jnp.bfloat16)

    def butterfly(table, source, m):
        a = jnp.dot(table[0], source[0, :, cols(m)], preferred_element_type=jnp.float32)
        b = jnp.dot(table[1], source[1, :, cols(m)], preferred_element_type=jnp.float32)
        return (a + b).astype(jnp.bfloat16), (a - b).astype(jnp.bfloat16)

    def spread_rows(m, row, lanes, value):
        size = min(GROUP, value.shape[0])
        for t in range(value.shape[0] // size):
            group, offset = divmod(row + t * size, GROUP)
            start = (group * modes + m) * GROUP + offset
            half[start : start + size, lanes] = value[t * size : (t + 1) * size]

    def columns(t, table):
        rows = slice(t * modes * GROUP, (t + 1) * modes * GROUP)
        return jnp.dot(half[rows, :], table[...], preferred_element_type=jnp.float32)

    first_lanes, last_lanes = slice(0, side), slice(side, 2 * side)
    for m in range(modes):
        for n, value in enumerate(butterfly(row_fwd_ref, psib, m)):
            spread_rows(m, n * hside, first_lanes, value[:hside])
            spread_rows(m, n * hside, last_lanes, value[hside:])
    for t in range(side // GROUP):
        product = columns(t, col_fwd_ref)
        for u in range(GROUP // CHUNK):
            i = t * (GROUP // CHUNK) + u
            parts = []
            energy = None
            for m in range(modes):
                here = slice(m * GROUP + u * CHUNK, m * GROUP + (u + 1) * CHUNK)
                a = product[here, :side]
                b = product[here, side:]
                e = a * a + b * b
                energy = e if energy is None else energy + e
                parts.append((a, b))
            group, offset = divmod(i * CHUNK, quarter)
            parity = group % 2
            place = group // 2 * quarter + offset
            measured = jnp.concatenate(
                [level[c, pl.ds(parity + 2 * place, CHUNK, stride=2), :] for c in range(side // 128)],
                axis=1,
            )
            fac = measured * lax.rsqrt(jnp.maximum(energy, 1.0))
            for m in range(modes):
                corr[parity, place : place + CHUNK, cols(m)] = (parts[m][0] * fac).astype(
                    jnp.bfloat16
                )
                corr[parity, hside + place : hside + place + CHUNK, cols(m)] = (
                    parts[m][1] * fac
                ).astype(jnp.bfloat16)
    for m in range(modes):
        for n, value in enumerate(butterfly(row_inv_ref, corr, m)):
            for w in range(2):
                row = w * hside + n * quarter
                spread_rows(m, row, first_lanes, value[w * quarter : (w + 1) * quarter])
                spread_rows(
                    m, row, last_lanes, value[hside + w * quarter : hside + (w + 1) * quarter]
                )
    for t in range(side // GROUP):
        product = columns(t, col_inv_ref)
        for u in range(GROUP // CHUNK):
            rows = slice(t * GROUP + u * CHUNK, t * GROUP + (u + 1) * CHUNK)
            o_r = patch[0, rows, :]
            o_i = patch[1, rows, :]
            power = power_ref[rows, :]
            g_r = -(o_r * power)
            g_i = -(o_i * power)
            for m in range(modes):
                here = slice(m * GROUP + u * CHUNK, m * GROUP + (u + 1) * CHUNK)
                a = product[here, :side]
                b = product[here, side:]
                pr = probe_ref[2 * m, rows, :]
                pi = probe_ref[2 * m + 1, rows, :]
                g_r += pr * a + pi * b
                g_i += pr * b - pi * a
                total[2 * m, rows, :] += o_r * a + o_i * b
                total[2 * m + 1, rows, :] += o_r * b - o_i * a
            grad[0, rows, :] = g_r
            grad[1, rows, :] = g_i
    for w in range(2):
        p, base, slide = line_start(w)
        for i in range(hside // PATCH):
            rows = slice(w * hside + i * PATCH, w * hside + (i + 1) * PATCH)
            here = pl.ds(base + i * PATCH, PATCH + 8)
            far = lane_tall >= shift
            none = jnp.zeros((8, 128), jnp.float32)
            for k in range(2):
                a, b = (
                    pltpu.roll(
                        pltpu.roll(
                            jnp.concatenate([grad[k, rows, strip_lanes(c)], none], axis=0), slide, 0
                        ),
                        shift,
                        1,
                    )
                    for c in range(2)
                )
                canvas[p, k, first, here, :] += jnp.where(far, a, 0.0)
                canvas[p, k, first + 1, here, :] += jnp.where(far, b, a)
                canvas[p, k, first + 2, here, :] += jnp.where(far, 0.0, b)

    @pl.when(f == count - 1)
    def _():
        step = step_ref[0]

        @pl.loop(0, lines // CHUNK)
        def _(i):
            rows = pl.ds(pl.multiple_of(i * CHUNK, CHUNK), CHUNK)
            inside = jnp.logical_and(i * CHUNK >= H // 2, i * CHUNK < (H + side) // 2)
            inside = inside.astype(jnp.float32)
            for p in range(2):
                target = pl.ds(2 * i * CHUNK + p, CHUNK, stride=2)
                for k in range(2):
                    for c in range(strips):
                        value = canvas[p, k, c + 1, rows, :]
                        if c == strips - 1:
                            value = step * (value + canvas[p, k, 0, rows, :])
                        else:
                            value = step * value + inside * field[p, k, c + 1, rows, :]
                        lined[k, c, target, :] = value

        @pl.loop(0, wide // CHUNK)
        def _(i):
            rows = pl.ds(pl.multiple_of(i * CHUNK, CHUNK), CHUNK)
            for k in range(2):
                for c in range(strips):
                    canvas_ref[k, rows, strip_lanes(c)] = lined[k, c, rows, :]

        planes = modes
        mine = core_ref[0] * planes
        theirs = planes - mine

        @pl.loop(0, side // 8)
        def _(i):
            rows = pl.ds(pl.multiple_of(i * 8, 8), 8)
            for j in range(side // 128):
                lanes = slice(j * 128, (j + 1) * 128)
                tile = i * (side // 128) + j
                for p in range(planes):
                    kept_ref[tile, p] = total[mine + p, rows, lanes]
                    other_ref[tile, p] = total[theirs + p, rows, lanes]
                kept_ref[tile, planes] = total[2 * modes, rows, lanes]
                other_ref[tile, planes] = total[2 * modes, rows, lanes]


def renew_kernel(spread_ref, old_ref, out_ref):
    modes = old_ref.shape[0]
    sums = [jnp.zeros((8, 128), jnp.float32) for _ in range(modes + 1)]
    for i in range(spread_ref.shape[0]):
        for p in range(modes + 1):
            sums[p] += spread_ref[i, p]
    weight = sums[modes]
    for p in range(modes):
        old = old_ref[p]
        new = old + (sums[p] - old * weight) / (weight + 1e-05)
        for i in range(out_ref.shape[0]):
            out_ref[i, p] = new


def renew(spread, old):
    return pl.pallas_call(
        renew_kernel,
        out_shape=jax.ShapeDtypeStruct(spread.shape[:1] + old.shape, jnp.float32),
        in_specs=[pl.BlockSpec(memory_space=pltpu.VMEM)] * 2,
        out_specs=pl.BlockSpec(memory_space=pltpu.VMEM),
        compiler_params=pltpu.CompilerParams(vmem_limit_bytes=8 * 1024 * 1024),
        cost_estimate=pl.CostEstimate(flops=0, bytes_accessed=2 * 2**20, transcendentals=0),
    )(spread, old)


def assemble_kernel(first_ref, source_ref, *refs):
    out_ref, lined = refs[-2:]
    plane = pl.program_id(0)
    side = out_ref.shape[1]
    lanes = side // 128
    for i in range(side // 8):
        parity, line = divmod(i * 8, side // 2)
        rows = pl.ds(2 * line + parity, 8, stride=2)
        for j in range(lanes):
            lined[j, rows, :] = source_ref[i * lanes + j, plane]
    for i in range(side // 8):
        rows = slice(i * 8, (i + 1) * 8)
        for j in range(lanes):
            out_ref[0, rows, j * 128 : (j + 1) * 128] = lined[j, rows, :]


def assemble(first, source, side, started=None):
    planes = source.shape[1]
    more = () if started is None else (started,)
    return pl.pallas_call(
        assemble_kernel,
        out_shape=jax.ShapeDtypeStruct((2 * planes, side, side), jnp.float32),
        grid_spec=pltpu.PrefetchScalarGridSpec(
            num_scalar_prefetch=1,
            grid=(planes,),
            in_specs=[
                pl.BlockSpec(source.shape, lambda p, *_: (0,) * source.ndim),
                *[pl.BlockSpec(memory_space=pl.ANY) for _ in more],
            ],
            out_specs=pl.BlockSpec(
                (1, side, side), lambda p, first_ref: (first_ref[0] + p, 0, 0)
            ),
            scratch_shapes=[pltpu.VMEM((side // 128, side, 128), jnp.float32)],
        ),
        input_output_aliases={2: 0} if more else {},
        compiler_params=pltpu.CompilerParams(vmem_limit_bytes=16 * 1024 * 1024),
        cost_estimate=pl.CostEstimate(flops=0, bytes_accessed=2 * 2**20, transcendentals=0),
    )(first, source, *more)


def frames(starts, core, step, ext, probe, power, amps, *tables):
    count, side, _ = amps.shape
    planes = probe.shape[0]
    modes = planes // 2
    wide = ext.shape[2]
    tiles = (side // 8) * (side // 128)

    def whole(shape):
        return pl.BlockSpec(shape, lambda f, *_: (0,) * len(shape))

    return pl.pallas_call(
        frames_kernel,
        out_shape=(
            jax.ShapeDtypeStruct((tiles, planes // 2 + 1, 8, 128), jnp.float32),
            jax.ShapeDtypeStruct((tiles, planes // 2 + 1, 8, 128), jnp.float32),
            jax.ShapeDtypeStruct((2, wide, wide), jnp.float32),
        ),
        grid_spec=pltpu.PrefetchScalarGridSpec(
            num_scalar_prefetch=3,
            grid=(count,),
            in_specs=[
                whole((2, wide, wide)),
                whole((planes, side, side)),
                whole((side, side)),
                pl.BlockSpec((1, side, side), lambda f, *_: (f, 0, 0)),
                *[whole(t.shape) for t in tables],
            ],
            out_specs=(
                whole((tiles, planes // 2 + 1, 8, 128)),
                whole((tiles, planes // 2 + 1, 8, 128)),
                whole((2, wide, wide)),
            ),
            scratch_shapes=[
                pltpu.VMEM((2, 2, wide // 128 + 1, wide // 2 + 8, 128), jnp.float32),
                pltpu.VMEM((2, side, side), jnp.float32),
                pltpu.VMEM((2, side, modes * side), jnp.bfloat16),
                pltpu.VMEM((modes * side, 2 * side), jnp.bfloat16),
                pltpu.VMEM((2, side, side), jnp.float32),
                pltpu.VMEM((2, side, modes * side), jnp.bfloat16),
                pltpu.VMEM((2, 2, wide // 128 + 1, wide // 2 + 8, 128), jnp.float32),
                pltpu.VMEM((planes + 1, side, side), jnp.float32),
                pltpu.VMEM((2, wide // 128, wide, 128), jnp.float32),
                pltpu.VMEM((side // 128, side, 128), jnp.float32),
            ],
        ),
        compiler_params=pltpu.CompilerParams(vmem_limit_bytes=34 * 1024 * 1024),
        cost_estimate=pl.CostEstimate(
            flops=count * modes * 4 * 8 * side**3, bytes_accessed=8 * 2**20, transcendentals=0
        ),
    )(starts, core, step, ext, probe, power, amps, *tables)


def exchange(low, high, axes):
    count = math.prod(lax.axis_size(a) for a in axes)
    even = lax.axis_index(axes) % 2 == 0
    pairs = [(i, i + 1) for i in range(0, count - 1, 2)]
    gaps = [(i, i + 1) for i in range(1, count - 1, 2)]
    inner = lax.ppermute(
        jnp.where(even, high, low), axes, pairs + [(j, i) for i, j in pairs]
    )
    outer = lax.ppermute(jnp.where(even, low, high), axes, gaps + [(j, i) for i, j in gaps])
    return jnp.where(even, outer, inner), jnp.where(even, inner, outer)


def packed(strip):
    return jnp.concatenate([strip[0], strip[1]], axis=1)


def unpacked(pack):
    width = pack.shape[1] // 2
    return jnp.stack([pack[:, :width], pack[:, width:]])


def shards(object_amplitude, object_phase, probe, amplitudes, positions):
    tile = object_amplitude.shape[0]
    side = probe.shape[2]
    own = jnp.stack([object_amplitude, object_phase])
    top, bottom = exchange(own[:, :H], own[:, tile - H :], ROW)
    tall = jnp.concatenate([top, own, bottom], axis=1)
    left, right = exchange(packed(tall[:, :, :H]), packed(tall[:, :, tile - H :]), COL)
    ext = jnp.concatenate([tall, unpacked(right), unpacked(left)], axis=2)

    planes = probe.reshape((-1, side // 2, 2, side)).swapaxes(1, 2).reshape((-1, side, side))
    power = jnp.sum(planes * planes, axis=0)
    step = 1.0 / (jnp.max(power) + 1e-06)
    core = lax.axis_index("c").astype(jnp.int32)
    kept, other, canvas = frames(
        positions.reshape((-1,)),
        core.reshape((1,)),
        step.reshape((1,)),
        ext,
        planes,
        power,
        amplitudes,
        *fourier_tables(side),
    )

    mine = planes.shape[0] // 2
    swap = [(0, 1), (1, 0)]
    both = kept + lax.ppermute(other, "c", swap)
    from_above, from_below = exchange(canvas[:, :H, :], canvas[:, H + tile :, :], ROW)
    both, from_above, from_below = lax.optimization_barrier((both, from_above, from_below))
    spread = lax.all_to_all(both, CHIPS, 0, 0, tiled=True)
    chip = lax.axis_index(CHIPS)
    lanes = side // 128
    old = lax.dynamic_slice(
        planes, (core * mine, chip // lanes * 8, chip % lanes * 128), (mine, 8, 128)
    )
    gathered = lax.all_to_all(renew(spread, old), CHIPS, 0, 0, tiled=True)
    centre = canvas[:, H : H + tile, :]
    centre = centre.at[:, :H].add(from_above)
    centre = centre.at[:, tile - H :].add(from_below)
    from_left, from_right = exchange(
        packed(centre[:, :, tile + H :]), packed(centre[:, :, tile : tile + H]), COL
    )
    from_left, from_right = unpacked(from_left), unpacked(from_right)
    inner = centre[:, :, :tile]
    inner = inner.at[:, :, :H].add(from_left)
    inner = inner.at[:, :, tile - H :].add(from_right)
    gathered, inner = lax.optimization_barrier((gathered, inner))
    swapped = lax.ppermute(gathered, "c", swap)
    first = (core * mine).reshape((1,))
    new_probe = assemble(first, gathered, side)
    new_probe = assemble(mine - first, swapped, side, new_probe)
    return (inner, new_probe.reshape(probe.shape))


def solution(mesh):
    fine = Mesh(mesh.devices.reshape((4, 2, 2, 4, 2)), ALL)
    in_specs = (
        P(ROW, COL),
        P(ROW, COL),
        P(),
        P(ALL, None, None),
        P(ALL, None),
    )
    out_specs = (P(None, ROW, COL), P())
    return jax.shard_map(shards, mesh=fine, in_specs=in_specs, out_specs=out_specs, check_vma=False)
```

```python
import functools
import math

import jax
import jax.numpy as jnp
import numpy as np
from jax import lax
from jax.experimental import pallas as pl
from jax.experimental.pallas import tpu as pltpu
from jax.sharding import Mesh, PartitionSpec as P

H = 64
ROW = ("z", "yh")
COL = ("yl", "x", "c")
CHIPS = ("z", "yh", "yl", "x")
ALL = CHIPS + ("c",)
CHUNK = 32
PATCH = 64
GROUP = 64


def real_form(table):
    return np.concatenate(
        [
            np.concatenate([table.real, -table.imag], axis=1),
            np.concatenate([table.imag, table.real], axis=1),
        ],
        axis=0,
    )


def fourier_tables(side):
    counter = np.arange(side, dtype=np.int64)
    angle = (counter[:, None] * counter[None, :] % side).astype(np.float64) * (2.0 * math.pi / side)
    table = (np.cos(angle) - 1j * np.sin(angle)) / math.sqrt(side)
    sorted_half = np.concatenate([counter[: side // 2 : 2], counter[1 : side // 2 : 2]])
    halves = table[sorted_half]
    row_fwd = np.stack([real_form(halves[:, p::2]) for p in range(2)])
    row_inv = np.stack([real_form(halves.conj()[:, p::2]) for p in range(2)])
    col_fwd = real_form(table).T
    col_inv = real_form(table.conj()).T
    return [jnp.asarray(t, dtype=jnp.bfloat16) for t in (row_fwd, col_fwd, row_inv, col_inv)]


def cosine_sine(angle):
    turns = jnp.floor(angle * (2.0 / math.pi) + 0.5)
    rest = ((angle - turns * 1.5703125) - turns * 4.837512969970703125e-4) - turns * 7.549789954e-8
    z = rest * rest
    s = ((-1.9515295891e-4 * z + 8.3321608736e-3) * z - 1.6666654611e-1) * z * rest + rest
    c = (
        ((2.443315711809948e-5 * z - 1.388731625493765e-3) * z + 4.166664568298827e-2) * z * z
        - 0.5 * z
        + 1.0
    )
    size = jnp.abs(turns)
    odd = size == 1.0
    sign = 1.0 - size
    return jnp.where(odd, -turns * s, sign * c), jnp.where(odd, turns * c, sign * s)


def frames_kernel(
    starts_ref,
    core_ref,
    step_ref,
    ext_ref,
    probe_ref,
    power_ref,
    amps_ref,
    row_fwd_ref,
    col_fwd_ref,
    row_inv_ref,
    col_inv_ref,
    kept_ref,
    other_ref,
    canvas_ref,
    field,
    patch,
    psib,
    half,
    grad,
    corr,
    canvas,
    total,
    lined,
    level,
):
    f = pl.program_id(0)
    count = pl.num_programs(0)
    modes = probe_ref.shape[0] // 2
    side = probe_ref.shape[1]
    wide = ext_ref.shape[2]
    hside = side // 2
    quarter = side // 4
    strips = wide // 128
    lines = wide // 2

    def strip_lanes(c):
        return slice(c * 128, (c + 1) * 128)

    @pl.when(f == 0)
    def _():
        zero = jnp.zeros((CHUNK, 128), jnp.float32)

        @pl.loop(0, wide // CHUNK)
        def _(i):
            rows = pl.ds(pl.multiple_of(i * CHUNK, CHUNK), CHUNK)
            for k in range(2):
                for c in range(strips):
                    lined[k, c, rows, :] = ext_ref[k, rows, strip_lanes(c)]

        @pl.loop(0, lines // CHUNK)
        def _(i):
            rows = pl.ds(pl.multiple_of(i * CHUNK, CHUNK), CHUNK)
            for p in range(2):
                source = pl.ds(2 * i * CHUNK + p, CHUNK, stride=2)
                for c in range(strips):
                    amp = lined[0, c, source, :]
                    cosine, sine = cosine_sine(lined[1, c, source, :])
                    for k, value in enumerate((amp * cosine, amp * sine)):
                        field[p, k, c + 1, rows, :] = value
                        if c == strips - 1:
                            field[p, k, 0, rows, :] = value
                for k in range(2):
                    for c in range(strips + 1):
                        canvas[p, k, c, rows, :] = zero

        for p in range(2):
            for k in range(2):
                for c in range(strips + 1):
                    field[p, k, c, lines:, :] = jnp.zeros((8, 128), jnp.float32)
                    canvas[p, k, c, lines:, :] = jnp.zeros((8, 128), jnp.float32)

        @pl.loop(0, side // CHUNK)
        def _(i):
            rows = pl.ds(pl.multiple_of(i * CHUNK, CHUNK), CHUNK)
            for p in range(2 * modes + 1):
                total[p, rows, :] = jnp.zeros((CHUNK, side), jnp.float32)

    r0 = starts_ref[2 * f] + H
    c0 = starts_ref[2 * f + 1]
    shift = jnp.where(c0 < 0, 128 + c0, c0)
    unshift = jnp.where(shift > 0, 128 - shift, 0)
    first = jnp.where(c0 < 0, 0, 1)
    lane_tall = lax.broadcasted_iota(jnp.int32, (PATCH + 8, 128), 1)

    for i in range(side // CHUNK):
        rows = slice(i * CHUNK, (i + 1) * CHUNK)
        for c in range(side // 128):
            level[c, rows, :] = amps_ref[0, rows, strip_lanes(c)]

    def cols(m):
        return slice(m * side, (m + 1) * side)

    def line_start(w):
        q = r0 + w
        index = q // 2
        slide = lax.rem(index, 8)
        return lax.rem(q, 2), pl.multiple_of(index - slide, 8), slide

    for w in range(2):
        p, base, slide = line_start(w)
        lift = lax.rem(PATCH + 8 - slide, PATCH + 8)
        for i in range(hside // PATCH):
            rows = slice(w * hside + i * PATCH, w * hside + (i + 1) * PATCH)
            o = []
            for k in range(2):
                turned = [
                    pltpu.roll(field[p, k, first + c, pl.ds(base + i * PATCH, PATCH + 8), :], unshift, 1)
                    for c in range(3)
                ]
                near = lane_tall < 128 - shift
                joined = [jnp.where(near, turned[c], turned[c + 1]) for c in range(2)]
                o.append(
                    jnp.concatenate([pltpu.roll(x, lift, 0)[:PATCH] for x in joined], axis=1)
                )
            patch[0, rows, :] = o[0]
            patch[1, rows, :] = o[1]
            total[2 * modes, rows, :] += o[0] * o[0] + o[1] * o[1]
            for m in range(modes):
                pr = probe_ref[2 * m, rows, :]
                pi = probe_ref[2 * m + 1, rows, :]
                psib[w, i * PATCH : (i + 1) * PATCH, cols(m)] = (pr * o[0] - pi * o[1]).astype(
                    jnp.bfloat16
                )
                psib[w, hside + i * PATCH : hside + (i + 1) * PATCH, cols(m)] = (
                    pr * o[1] + pi * o[0]
                ).astype(jnp.bfloat16)

    def butterfly(table, source, m):
        a = jnp.dot(table[0], source[0, :, cols(m)], preferred_element_type=jnp.float32)
        b = jnp.dot(table[1], source[1, :, cols(m)], preferred_element_type=jnp.float32)
        return (a + b).astype(jnp.bfloat16), (a - b).astype(jnp.bfloat16)

    def spread_rows(m, row, lanes, value):
        size = min(GROUP, value.shape[0])
        for t in range(value.shape[0] // size):
            group, offset = divmod(row + t * size, GROUP)
            start = (group * modes + m) * GROUP + offset
            half[start : start + size, lanes] = value[t * size : (t + 1) * size]

    def columns(t, table):
        rows = slice(t * modes * GROUP, (t + 1) * modes * GROUP)
        return jnp.dot(half[rows, :], table[...], preferred_element_type=jnp.float32)

    first_lanes, last_lanes = slice(0, side), slice(side, 2 * side)
    for m in range(modes):
        for n, value in enumerate(butterfly(row_fwd_ref, psib, m)):
            spread_rows(m, n * hside, first_lanes, value[:hside])
            spread_rows(m, n * hside, last_lanes, value[hside:])
    for t in range(side // GROUP):
        product = columns(t, col_fwd_ref)
        for u in range(GROUP // CHUNK):
            i = t * (GROUP // CHUNK) + u
            parts = []
            energy = None
            for m in range(modes):
                here = slice(m * GROUP + u * CHUNK, m * GROUP + (u + 1) * CHUNK)
                a = product[here, :side]
                b = product[here, side:]
                e = a * a + b * b
                energy = e if energy is None else energy + e
                parts.append((a, b))
            group, offset = divmod(i * CHUNK, quarter)
            parity = group % 2
            place = group // 2 * quarter + offset
            measured = jnp.concatenate(
                [level[c, pl.ds(parity + 2 * place, CHUNK, stride=2), :] for c in range(side // 128)],
                axis=1,
            )
            fac = measured * lax.rsqrt(jnp.maximum(energy, 1.0))
            for m in range(modes):
                corr[parity, place : place + CHUNK, cols(m)] = (parts[m][0] * fac).astype(
                    jnp.bfloat16
                )
                corr[parity, hside + place : hside + place + CHUNK, cols(m)] = (
                    parts[m][1] * fac
                ).astype(jnp.bfloat16)
    for m in range(modes):
        for n, value in enumerate(butterfly(row_inv_ref, corr, m)):
            for w in range(2):
                row = w * hside + n * quarter
                spread_rows(m, row, first_lanes, value[w * quarter : (w + 1) * quarter])
                spread_rows(
                    m, row, last_lanes, value[hside + w * quarter : hside + (w + 1) * quarter]
                )
    for t in range(side // GROUP):
        product = columns(t, col_inv_ref)
        for u in range(GROUP // CHUNK):
            rows = slice(t * GROUP + u * CHUNK, t * GROUP + (u + 1) * CHUNK)
            o_r = patch[0, rows, :]
            o_i = patch[1, rows, :]
            power = power_ref[rows, :]
            g_r = -(o_r * power)
            g_i = -(o_i * power)
            for m in range(modes):
                here = slice(m * GROUP + u * CHUNK, m * GROUP + (u + 1) * CHUNK)
                a = product[here, :side]
                b = product[here, side:]
                pr = probe_ref[2 * m, rows, :]
                pi = probe_ref[2 * m + 1, rows, :]
                g_r += pr * a + pi * b
                g_i += pr * b - pi * a
                total[2 * m, rows, :] += o_r * a + o_i * b
                total[2 * m + 1, rows, :] += o_r * b - o_i * a
            grad[0, rows, :] = g_r
            grad[1, rows, :] = g_i
    for w in range(2):
        p, base, slide = line_start(w)
        for i in range(hside // PATCH):
            rows = slice(w * hside + i * PATCH, w * hside + (i + 1) * PATCH)
            here = pl.ds(base + i * PATCH, PATCH + 8)
            far = lane_tall >= shift
            none = jnp.zeros((8, 128), jnp.float32)
            for k in range(2):
                a, b = (
                    pltpu.roll(
                        pltpu.roll(
                            jnp.concatenate([grad[k, rows, strip_lanes(c)], none], axis=0), slide, 0
                        ),
                        shift,
                        1,
                    )
                    for c in range(2)
                )
                canvas[p, k, first, here, :] += jnp.where(far, a, 0.0)
                canvas[p, k, first + 1, here, :] += jnp.where(far, b, a)
                canvas[p, k, first + 2, here, :] += jnp.where(far, 0.0, b)

    @pl.when(f == count - 1)
    def _():
        step = step_ref[0]

        @pl.loop(0, lines // CHUNK)
        def _(i):
            rows = pl.ds(pl.multiple_of(i * CHUNK, CHUNK), CHUNK)
            inside = jnp.logical_and(i * CHUNK >= H // 2, i * CHUNK < (H + side) // 2)
            inside = inside.astype(jnp.float32)
            for p in range(2):
                target = pl.ds(2 * i * CHUNK + p, CHUNK, stride=2)
                for k in range(2):
                    for c in range(strips):
                        value = canvas[p, k, c + 1, rows, :]
                        if c == strips - 1:
                            value = step * (value + canvas[p, k, 0, rows, :])
                        else:
                            value = step * value + inside * field[p, k, c + 1, rows, :]
                        lined[k, c, target, :] = value

        @pl.loop(0, wide // CHUNK)
        def _(i):
            rows = pl.ds(pl.multiple_of(i * CHUNK, CHUNK), CHUNK)
            for k in range(2):
                for c in range(strips):
                    canvas_ref[k, rows, strip_lanes(c)] = lined[k, c, rows, :]

        planes = modes
        mine = core_ref[0] * planes
        theirs = planes - mine

        @pl.loop(0, side // 8)
        def _(i):
            rows = pl.ds(pl.multiple_of(i * 8, 8), 8)
            for j in range(side // 128):
                lanes = slice(j * 128, (j + 1) * 128)
                tile = i * (side // 128) + j
                for p in range(planes):
                    kept_ref[tile, p] = total[mine + p, rows, lanes]
                    other_ref[tile, p] = total[theirs + p, rows, lanes]
                kept_ref[tile, planes] = total[2 * modes, rows, lanes]
                other_ref[tile, planes] = total[2 * modes, rows, lanes]


def renew_kernel(spread_ref, old_ref, out_ref):
    modes = old_ref.shape[0]
    sums = [jnp.zeros((8, 128), jnp.float32) for _ in range(modes + 1)]
    for i in range(spread_ref.shape[0]):
        for p in range(modes + 1):
            sums[p] += spread_ref[i, p]
    weight = sums[modes]
    for p in range(modes):
        old = old_ref[p]
        new = old + (sums[p] - old * weight) / (weight + 1e-05)
        for i in range(out_ref.shape[0]):
            out_ref[i, p] = new


def renew(spread, old):
    return pl.pallas_call(
        renew_kernel,
        out_shape=jax.ShapeDtypeStruct(spread.shape[:1] + old.shape, jnp.float32),
        in_specs=[pl.BlockSpec(memory_space=pltpu.VMEM)] * 2,
        out_specs=pl.BlockSpec(memory_space=pltpu.VMEM),
        compiler_params=pltpu.CompilerParams(vmem_limit_bytes=8 * 1024 * 1024),
        cost_estimate=pl.CostEstimate(flops=0, bytes_accessed=2 * 2**20, transcendentals=0),
    )(spread, old)


def assemble_kernel(first_ref, source_ref, *refs):
    out_ref, lined = refs[-2:]
    plane = pl.program_id(0)
    side = out_ref.shape[1]
    lanes = side // 128
    for i in range(side // 8):
        parity, line = divmod(i * 8, side // 2)
        rows = pl.ds(2 * line + parity, 8, stride=2)
        for j in range(lanes):
            lined[j, rows, :] = source_ref[i * lanes + j, plane]
    for i in range(side // 8):
        rows = slice(i * 8, (i + 1) * 8)
        for j in range(lanes):
            out_ref[0, rows, j * 128 : (j + 1) * 128] = lined[j, rows, :]


def assemble(first, source, side, started=None):
    planes = source.shape[1]
    more = () if started is None else (started,)
    return pl.pallas_call(
        assemble_kernel,
        out_shape=jax.ShapeDtypeStruct((2 * planes, side, side), jnp.float32),
        grid_spec=pltpu.PrefetchScalarGridSpec(
            num_scalar_prefetch=1,
            grid=(planes,),
            in_specs=[
                pl.BlockSpec(source.shape, lambda p, *_: (0,) * source.ndim),
                *[pl.BlockSpec(memory_space=pl.ANY) for _ in more],
            ],
            out_specs=pl.BlockSpec(
                (1, side, side), lambda p, first_ref: (first_ref[0] + p, 0, 0)
            ),
            scratch_shapes=[pltpu.VMEM((side // 128, side, 128), jnp.float32)],
        ),
        input_output_aliases={2: 0} if more else {},
        compiler_params=pltpu.CompilerParams(vmem_limit_bytes=16 * 1024 * 1024),
        cost_estimate=pl.CostEstimate(flops=0, bytes_accessed=2 * 2**20, transcendentals=0),
    )(first, source, *more)


def frames(starts, core, step, ext, probe, power, amps, *tables):
    count, side, _ = amps.shape
    planes = probe.shape[0]
    modes = planes // 2
    wide = ext.shape[2]
    tiles = (side // 8) * (side // 128)

    def whole(shape):
        return pl.BlockSpec(shape, lambda f, *_: (0,) * len(shape))

    return pl.pallas_call(
        frames_kernel,
        out_shape=(
            jax.ShapeDtypeStruct((tiles, planes // 2 + 1, 8, 128), jnp.float32),
            jax.ShapeDtypeStruct((tiles, planes // 2 + 1, 8, 128), jnp.float32),
            jax.ShapeDtypeStruct((2, wide, wide), jnp.float32),
        ),
        grid_spec=pltpu.PrefetchScalarGridSpec(
            num_scalar_prefetch=3,
            grid=(count,),
            in_specs=[
                whole((2, wide, wide)),
                whole((planes, side, side)),
                whole((side, side)),
                pl.BlockSpec((1, side, side), lambda f, *_: (f, 0, 0)),
                *[whole(t.shape) for t in tables],
            ],
            out_specs=(
                whole((tiles, planes // 2 + 1, 8, 128)),
                whole((tiles, planes // 2 + 1, 8, 128)),
                whole((2, wide, wide)),
            ),
            scratch_shapes=[
                pltpu.VMEM((2, 2, wide // 128 + 1, wide // 2 + 8, 128), jnp.float32),
                pltpu.VMEM((2, side, side), jnp.float32),
                pltpu.VMEM((2, side, modes * side), jnp.bfloat16),
                pltpu.VMEM((modes * side, 2 * side), jnp.bfloat16),
                pltpu.VMEM((2, side, side), jnp.float32),
                pltpu.VMEM((2, side, modes * side), jnp.bfloat16),
                pltpu.VMEM((2, 2, wide // 128 + 1, wide // 2 + 8, 128), jnp.float32),
                pltpu.VMEM((planes + 1, side, side), jnp.float32),
                pltpu.VMEM((2, wide // 128, wide, 128), jnp.float32),
                pltpu.VMEM((side // 128, side, 128), jnp.float32),
            ],
        ),
        compiler_params=pltpu.CompilerParams(vmem_limit_bytes=34 * 1024 * 1024),
        cost_estimate=pl.CostEstimate(
            flops=count * modes * 4 * 8 * side**3, bytes_accessed=8 * 2**20, transcendentals=0
        ),
    )(starts, core, step, ext, probe, power, amps, *tables)


def exchange(low, high, axes):
    count = math.prod(lax.axis_size(a) for a in axes)
    even = lax.axis_index(axes) % 2 == 0
    pairs = [(i, i + 1) for i in range(0, count - 1, 2)]
    gaps = [(i, i + 1) for i in range(1, count - 1, 2)]
    inner = lax.ppermute(
        jnp.where(even, high, low), axes, pairs + [(j, i) for i, j in pairs]
    )
    outer = lax.ppermute(jnp.where(even, low, high), axes, gaps + [(j, i) for i, j in gaps])
    return jnp.where(even, outer, inner), jnp.where(even, inner, outer)


def packed(strip):
    return jnp.concatenate([strip[0], strip[1]], axis=1)


def unpacked(pack):
    width = pack.shape[1] // 2
    return jnp.stack([pack[:, :width], pack[:, width:]])


def shards(object_amplitude, object_phase, probe, amplitudes, positions):
    tile = object_amplitude.shape[0]
    side = probe.shape[2]
    own = jnp.stack([object_amplitude, object_phase])
    top, bottom = exchange(own[:, :H], own[:, tile - H :], ROW)
    tall = jnp.concatenate([top, own, bottom], axis=1)
    left, right = exchange(packed(tall[:, :, :H]), packed(tall[:, :, tile - H :]), COL)
    ext = jnp.concatenate([tall, unpacked(right), unpacked(left)], axis=2)

    planes = probe.reshape((-1, side // 2, 2, side)).swapaxes(1, 2).reshape((-1, side, side))
    power = jnp.sum(planes * planes, axis=0)
    step = 1.0 / (jnp.max(power) + 1e-06)
    core = lax.axis_index("c").astype(jnp.int32)
    kept, other, canvas = frames(
        positions.reshape((-1,)),
        core.reshape((1,)),
        step.reshape((1,)),
        ext,
        planes,
        power,
        amplitudes,
        *fourier_tables(side),
    )

    mine = planes.shape[0] // 2
    swap = [(0, 1), (1, 0)]
    both = kept + lax.ppermute(other, "c", swap)
    from_above, from_below = exchange(canvas[:, :H, :], canvas[:, H + tile :, :], ROW)
    both, from_above, from_below = lax.optimization_barrier((both, from_above, from_below))
    spread = lax.all_to_all(both, CHIPS, 0, 0, tiled=True)
    chip = lax.axis_index(CHIPS)
    lanes = side // 128
    old = lax.dynamic_slice(
        planes, (core * mine, chip // lanes * 8, chip % lanes * 128), (mine, 8, 128)
    )
    gathered = lax.all_to_all(renew(spread, old), CHIPS, 0, 0, tiled=True)
    centre = canvas[:, H : H + tile, :]
    centre = centre.at[:, :H].add(from_above)
    centre = centre.at[:, tile - H :].add(from_below)
    from_left, from_right = exchange(
        packed(centre[:, :, tile + H :]), packed(centre[:, :, tile : tile + H]), COL
    )
    from_left, from_right = unpacked(from_left), unpacked(from_right)
    inner = centre[:, :, :tile]
    inner = inner.at[:, :, :H].add(from_left)
    inner = inner.at[:, :, tile - H :].add(from_right)
    gathered, inner = lax.optimization_barrier((gathered, inner))
    swapped = lax.ppermute(gathered, "c", swap)
    first = (core * mine).reshape((1,))
    new_probe = assemble(first, gathered, side)
    new_probe = assemble(mine - first, swapped, side, new_probe)
    return (inner, new_probe.reshape(probe.shape))


def solution(mesh):
    fine = Mesh(mesh.devices.reshape((4, 2, 2, 4, 2)), ALL)
    in_specs = (
        P(ROW, COL),
        P(ROW, COL),
        P(),
        P(ALL, None, None),
        P(ALL, None),
    )
    out_specs = (P(None, ROW, COL), P())
    return jax.shard_map(shards, mesh=fine, in_specs=in_specs, out_specs=out_specs, check_vma=False)
```
